32 devices in a mesh: db: 16 (over z, y, x), head: 2 (over core).
Axes of the slice: x: 2, y: 2, z: 4, core: 2. Of those that a mesh axis runs over, the one named last changes fastest.
Arguments:
- queries: bfloat16 [2048, 4096], P('db', 'head'), may hold values from -6 to 6
- w_key: bfloat16 [896, 4096], P(None, 'head'), may hold values from -0.1875 to 0.1875
- w_value: bfloat16 [896, 4096], P(None, 'head'), may hold values from -0.1875 to 0.1875
- w_out: bfloat16 [4096, 4096], P('head'), may hold values from -0.375 to 0.375
- encodings: bfloat16 [1024, 128, 896], P('db', 'head'), may hold values from -6 to 6
- nbr_row: int32 [32, 8], P('db'), may hold values from 0 to 63
- nbr_owner: int32 [32, 8], P('db'), may hold values from 0 to 15, all different within a row; in each aligned block of 2 rows (0 to 1, 2 to 3, ...) at most 2 rows name the same one
- nbr_count: int32 [32], P('db'), may hold values from 2 to 8
- grad_out: bfloat16 [2048, 4096], P('db', 'head'), may hold values from -6 to 6
Outputs:
- attended: bfloat16 [2048, 4096], P('db', 'head')
- grad_queries: bfloat16 [2048, 4096], P('db', 'head')
- grad_wk: float32 [896, 4096], P('db', 'head')
- grad_wv: float32 [896, 4096], P('db', 'head')
- grad_wo: float32 [4096, 4096], P('head', 'db')
The draws below stay inside these ranges and needn't reach their ends.
Inputs may be any that keep to these rules, and one draw needn't show every extreme that they name: `nbr_owner`: the 8 owners named by one group are all different.
All inputs are finite; a program needn't handle non-finite values.
Results may differ from the reference program's by a relative error of at most 0.023.
Values may be sent and summed in bfloat16 or wider, within the bound.
A program may use at most 192 MiB of HBM per device.

```python
import math
import jax
import jax.numpy as jnp
import numpy as np
from jax import lax

D = 4096
HEADS = 32
HD = 128
E = 896
NT = 128
CL = 64
K = 8
CH_DEV = 2
NB_DEV = 64
GROUPS = 32
TOKENS = 2048
NBR = 1024
N_DB = 16


def plant(drawn, rng, low, top_value):
    index_at = [jax.random.randint(jax.random.fold_in(rng, axis), (), 0, length) for axis, length in enumerate(drawn.shape)]
    widest = drawn.shape.index(max(drawn.shape))
    next_to = index_at[:widest] + [(index_at[widest] + 1) % drawn.shape[widest]] + index_at[widest + 1:]
    return drawn.at[tuple(index_at)].set(low).at[tuple(next_to)].set(top_value)


def strengthened(array, rng, source, target, shards_of, factor):
    def block_of(axis_at):
        return (jnp.arange(array.shape[axis_at]) // (array.shape[axis_at] // shards_of)).reshape((-1,) + (1,) * (array.ndim - 1 - axis_at))

    first = jax.random.permutation(rng, shards_of)[block_of(target)]
    second = (block_of(target) + shards_of // 2) % shards_of
    return jnp.where((block_of(source) == first) | (block_of(source) == second), factor * array, array)


def block_levels(own_key, extent, shards, least, high):
    def one(position, blocks):
        draws = jax.random.uniform(jax.random.fold_in(jax.random.fold_in(own_key, 6), position), (blocks,), jnp.float32, least / len(shards), high / len(shards))
        return jnp.repeat(jnp.exp(draws), extent[position] // blocks).reshape((-1,) + (1,) * (len(extent) - position - 1))

    gain = one(*shards[0])
    for cut in shards[1:]:
        gain = gain * one(*cut)
    return gain


def deal_out(key, own, number, rows, amount, top, reach, lean):
    order = jax.random.permutation(key, amount)
    packed, common = shares(amount, rows * top, reach, lean, True), shares(amount, rows * top, reach, lean, False)
    places = jnp.arange(amount)

    def named(tallies, turn):
        used = int((tallies > 0).sum())
        fixed = max(1, used // 4)
        shifted = fixed + (places - fixed + turn * (used - fixed)) % max(1, amount - fixed)
        return jnp.zeros((amount,), jnp.int32).at[order[jnp.where(places < fixed, places, shifted)]].set(jnp.asarray(tallies, jnp.int32))

    tallies = jnp.where(number % 4 == 0, named(packed, number // 4), named(common, number - number // 4 - 1))
    mixed = jax.random.permutation(jax.random.fold_in(own, 3), amount)
    source_of, receiver = mixed[0:amount // 2 * 2:2], mixed[1:amount // 2 * 2:2]
    margin = jnp.minimum(tallies[source_of] - 1, reach - tallies[receiver]) // 2
    margin = jnp.where((source_of == order[0]) | (receiver == order[0]) | (tallies[receiver] == 0), 0, jnp.maximum(margin, 0))
    shifted = jax.random.randint(jax.random.fold_in(own, 4), (amount // 2,), 0, 1 << 20) % (margin + 1)
    tallies = tallies.at[source_of].add(-shifted).at[receiver].add(shifted)
    labels = jnp.searchsorted(jnp.cumsum(tallies), jnp.arange(rows * top), side="right").astype(jnp.int32)
    grid = labels.reshape(top, rows).T
    grid = grid[jax.random.permutation(jax.random.fold_in(own, 1), rows)]
    turn = jax.random.randint(jax.random.fold_in(own, 2), (rows, 1), 0, top)
    return jnp.take_along_axis(grid, (jnp.arange(top)[None, :] + turn) % top, axis=1)


def shares(number_of, total, reach, lean, full):
    portions = [(1 << 20) // math.isqrt(grade ** lean) + 1 for grade in range(1, number_of + 1)]
    largest = reach if full else min(reach, max(-(-total // number_of), total * portions[0] // sum(portions)))
    least = 1 if total - largest >= number_of - 1 else 0
    given, rest = [largest] + [least] * (number_of - 1), total - largest - least * (number_of - 1)
    while rest > 0:
        movable = [i for i in range(1, number_of) if given[i] < largest] or [i for i in range(1, number_of) if given[i] < reach]
        mass, budget = sum([portions[i] for i in movable]), rest
        for i in movable:
            addition = min(reach - given[i], max(1, budget * portions[i] // mass), rest)
            given[i] = given[i] + addition
            rest = rest - addition
    return np.array(given)


def centred(rng, extent, deviation, limit, cuts=(), kind=jnp.bfloat16):
    result = jax.random.normal(rng, extent, jnp.float32) * deviation
    if len(cuts) > 0:
        result = block_levels(rng, extent, cuts, -0.22, 0.18) * result
    return jnp.clip(result, min=-limit, max=limit).astype(kind)


def noise_with(own_key, shape, deviation, reach, shards, heavy, held_as=jnp.bfloat16):
    values = deviation * jax.random.normal(own_key, shape, jnp.float32)
    if shards:
        values = values * block_levels(own_key, shape, shards, -0.22, 0.18)
    return jnp.clip(strengthened(values, jax.random.fold_in(own_key, 3), *heavy), -reach, reach).astype(held_as)


def setup_inputs(seed: int = 0) -> dict:
    splits = jax.random.split(jax.random.key(seed), 10)
    queries = centred(splits[0], (TOKENS, D), 1.0, 6.0, ((0, 16), (1, 2)))
    w_key = centred(splits[1], (E, D), E ** -0.5, 0.1875, ((1, 2),))
    w_value = centred(splits[2], (E, D), E ** -0.5, 0.1875, ((1, 2),))
    w_out = centred(splits[3], (D, D), (D // 16) ** -0.5, 0.375, ((0, 2),))
    encodings = centred(splits[4], (NBR, NT, E), 1.0, 6.0, ((0, 16), (1, 2)))
    nbr_row = plant(jax.random.randint(splits[5], (GROUPS, K), 0, NB_DEV), jax.random.fold_in(splits[5], 1), 0, NB_DEV - 1).astype(jnp.int32)
    nbr_owner_keys = jax.random.split(jax.random.fold_in(splits[6], 1), GROUPS // CH_DEV)
    nbr_owner_turns = jax.random.permutation(jax.random.fold_in(splits[6], 3), GROUPS // CH_DEV)
    nbr_owner = jax.vmap(lambda own, number: deal_out(jax.random.fold_in(splits[6], 2), own, number, CH_DEV, N_DB, K, CH_DEV, 1))(nbr_owner_keys, nbr_owner_turns).reshape((GROUPS, K))
    nbr_count = plant(jax.random.randint(splits[7], (GROUPS,), 2, K + 1), jax.random.fold_in(splits[7], 1), 2, K).astype(jnp.int32)
    grad_out = noise_with(splits[8], (TOKENS, D), 1.0, 6.0, ((0, 16), (1, 2)), (0, 1, 16, 2.0))
    return dict(queries=queries, w_key=w_key, w_value=w_value, w_out=w_out, encodings=encodings, nbr_row=nbr_row, nbr_owner=nbr_owner, nbr_count=nbr_count, grad_out=grad_out)


def rounded(value):
    return lax.optimization_barrier(value.astype(jnp.bfloat16))

def reference(queries, w_key, w_value, w_out, encodings, nbr_row, nbr_owner, nbr_count, grad_out):
    factor = 1.0 / math.sqrt(HD)
    global_rows = (nbr_owner * NB_DEV + nbr_row).astype(jnp.int32)
    query_blocks = queries.reshape(GROUPS, CL, D)
    cotangent_blocks = grad_out.reshape(GROUPS, CL, D)

    def one_group(carry, inputs):
        acc_key, acc_value, acc_out = carry
        query_group, grad_group, row_ids, count = inputs
        slots = jnp.take(encodings, row_ids, axis=0).reshape(K * NT, E)
        keys = rounded(jnp.dot(slots, w_key, preferred_element_type=jnp.float32))
        values = rounded(jnp.dot(slots, w_value, preferred_element_type=jnp.float32))
        query_heads = query_group.astype(jnp.float32).reshape(CL, HEADS, HD)
        key_heads = keys.astype(jnp.float32).reshape(K * NT, HEADS, HD)
        value_heads = values.astype(jnp.float32).reshape(K * NT, HEADS, HD)
        scores = jnp.einsum('qhd,khd->hqk', query_heads, key_heads) * factor
        live = jnp.arange(K * NT, dtype=jnp.int32) // NT < count
        expo = jnp.where(live[None, None, :], jnp.exp(scores), jnp.float32(0.0))
        probs = expo / lax.optimization_barrier(jnp.sum(expo, axis=-1, keepdims=True))
        probs_b = rounded(probs).astype(jnp.float32)
        mixed = rounded(jnp.einsum('hqk,khd->qhd', probs_b, value_heads)).reshape(CL, D)
        output = jnp.dot(mixed, w_out, preferred_element_type=jnp.float32).astype(jnp.bfloat16)
        d_mixed = rounded(jnp.dot(grad_group, w_out.T, preferred_element_type=jnp.float32))
        acc_out = acc_out + jnp.dot(mixed.T, grad_group, preferred_element_type=jnp.float32)
        d_mixed_heads = d_mixed.astype(jnp.float32).reshape(CL, HEADS, HD)
        d_probs = jnp.einsum('qhd,khd->hqk', d_mixed_heads, value_heads)
        inner = lax.optimization_barrier(jnp.sum(probs * d_probs, axis=-1, keepdims=True))
        d_scores = rounded(probs * (d_probs - inner) * factor).astype(jnp.float32)
        d_query = jnp.einsum('hqk,khd->qhd', d_scores, key_heads).astype(jnp.bfloat16).reshape(CL, D)
        d_keys = jnp.einsum('hqk,qhd->khd', d_scores, query_heads).astype(jnp.bfloat16).reshape(K * NT, D)
        d_values = jnp.einsum('hqk,qhd->khd', probs_b, d_mixed_heads).astype(jnp.bfloat16).reshape(K * NT, D)
        acc_key = acc_key + jnp.dot(slots.T, d_keys, preferred_element_type=jnp.float32)
        acc_value = acc_value + jnp.dot(slots.T, d_values, preferred_element_type=jnp.float32)
        return ((acc_key, acc_value, acc_out), (output, d_query))
    start = (jnp.zeros((E, D), jnp.float32), jnp.zeros((E, D), jnp.float32), jnp.zeros((D, D), jnp.float32))
    totals, pieces = lax.scan(one_group, start, (query_blocks, cotangent_blocks, global_rows, nbr_count))
    attended = pieces[0].reshape(TOKENS, D)
    grad_queries = pieces[1].reshape(TOKENS, D)
    return (attended, grad_queries, totals[0], totals[1], totals[2])
```

```python
import functools
import math

import jax
import jax.numpy as jnp
from jax import lax
from jax.experimental import pallas as pl
from jax.experimental.pallas import tpu as pltpu
from jax.sharding import PartitionSpec as P

HD = 128
F32 = jnp.float32
BF16 = jnp.bfloat16
VMEM_LIMIT = 56 * 1024 * 1024


def nt(a, b):
    return lax.dot_general(a, b, (((1,), (1,)), ((), ())), preferred_element_type=F32)


def nn(a, b):
    return jnp.dot(a, b, preferred_element_type=F32)


def tn(a, b):
    return lax.dot_general(a, b, (((0,), (0,)), ((), ())), preferred_element_type=F32)


def forward_kernel(groups, heads, count_ref, slots_ref, q_ref, dm_ref, wk_ref, wv_ref,
                   mixed_ref, probs_ref, gwv_ref, pulled_ref):
    tokens = q_ref.shape[0] // groups
    key_len = slots_ref.shape[1]
    tokens_per_slot = key_len // 8
    factor = 1.0 / math.sqrt(HD)
    for c in range(groups):
        rows = slice(c * tokens, (c + 1) * tokens)
        slots = slots_ref[c]
        lifted = jnp.concatenate(
            [
                nt(q_ref[rows, h * HD:(h + 1) * HD], wk_ref[:, h * HD:(h + 1) * HD]).astype(BF16)
                for h in range(heads)
            ],
            axis=0,
        )
        scores = nt(lifted, slots) * factor
        position = lax.broadcasted_iota(jnp.int32, (1, key_len), 1)
        live = position < count_ref[c] * tokens_per_slot
        expo = jnp.where(live, jnp.exp(scores), 0.0)
        probs = (expo / jnp.sum(expo, axis=-1, keepdims=True)).astype(BF16)
        probs_ref[0, c] = probs
        pulled = nn(probs, slots).astype(BF16)
        for h in range(heads):
            part = pulled[h * tokens:(h + 1) * tokens]
            cols = slice(h * HD, (h + 1) * HD)
            mixed_ref[rows, cols] = nn(part, wv_ref[:, cols]).astype(BF16)
            pulled_ref[h, rows, :] = part
    for h in range(heads):
        cols = slice(h * HD, (h + 1) * HD)
        gwv_ref[:, cols] = tn(pulled_ref[h], dm_ref[:, cols]).astype(BF16)


def backward_kernel(groups, heads, slots_ref, q_ref, dm_ref, wk_ref, wv_ref, probs_ref,
                    gq_ref, gwk_ref, pulled_ref):
    tokens = q_ref.shape[0] // groups
    factor = 1.0 / math.sqrt(HD)
    for c in range(groups):
        rows = slice(c * tokens, (c + 1) * tokens)
        slots = slots_ref[c]
        lifted = jnp.concatenate(
            [
                nt(dm_ref[rows, h * HD:(h + 1) * HD], wv_ref[:, h * HD:(h + 1) * HD]).astype(BF16)
                for h in range(heads)
            ],
            axis=0,
        )
        d_probs = nt(lifted, slots)
        probs = probs_ref[0, c].astype(F32)
        weighted = probs * d_probs
        inner = jnp.sum(weighted, axis=-1, keepdims=True)
        d_scores = ((weighted - probs * inner) * factor).astype(BF16)
        pulled = nn(d_scores, slots).astype(BF16)
        for h in range(heads):
            part = pulled[h * tokens:(h + 1) * tokens]
            cols = slice(h * HD, (h + 1) * HD)
            gq_ref[rows, cols] = nn(part, wk_ref[:, cols]).astype(BF16)
            pulled_ref[h, rows, :] = part
    for h in range(heads):
        cols = slice(h * HD, (h + 1) * HD)
        gwk_ref[:, cols] = tn(pulled_ref[h], q_ref[:, cols]).astype(BF16)


def attention_calls(slots, queries, d_mixed, w_key, w_value, nbr_count):
    groups, key_len, enc = slots.shape
    tok_rows, width = queries.shape
    heads = min(4, width // HD)
    steps = width // (heads * HD)
    part = heads * HD
    group_rows = heads * (tok_rows // groups)
    whole = pl.BlockSpec((groups, key_len, enc), lambda i: (0, 0, 0))
    tok = pl.BlockSpec((tok_rows, part), lambda i: (0, i))
    weight = pl.BlockSpec((enc, part), lambda i: (0, i))
    prob = pl.BlockSpec((1, groups, group_rows, key_len), lambda i: (i, 0, 0, 0))
    tok_shape = jax.ShapeDtypeStruct((tok_rows, width), BF16)
    weight_shape = jax.ShapeDtypeStruct((enc, width), BF16)
    prob_shape = jax.ShapeDtypeStruct((steps, groups, group_rows, key_len), BF16)
    cost = pl.CostEstimate(
        flops=int(4 * groups * group_rows * key_len * enc * steps * 1.2),
        bytes_accessed=20_000_000,
        transcendentals=groups * group_rows * steps * key_len,
    )
    common = dict(
        grid=(steps,),
        scratch_shapes=[pltpu.VMEM((heads, tok_rows, enc), BF16)],
        compiler_params=pltpu.CompilerParams(vmem_limit_bytes=VMEM_LIMIT),
        cost_estimate=cost,
    )
    mixed, probs, gwv = pl.pallas_call(
        functools.partial(forward_kernel, groups, heads),
        in_specs=[pl.BlockSpec(memory_space=pltpu.SMEM), whole, tok, tok, weight, weight],
        out_specs=[tok, prob, weight],
        out_shape=[tok_shape, prob_shape, weight_shape],
        **common,
    )(nbr_count, slots, queries, d_mixed, w_key, w_value)
    gq, gwk = pl.pallas_call(
        functools.partial(backward_kernel, groups, heads),
        in_specs=[whole, tok, tok, weight, weight, prob],
        out_specs=[tok, weight],
        out_shape=[tok_shape, weight_shape],
        **common,
    )(slots, queries, d_mixed, w_key, w_value, probs)
    return mixed, gwv, gq, gwk


def shards(queries, w_key, w_value, w_out, encodings, nbr_row, nbr_owner, nbr_count, grad_out):
    db_count = lax.axis_size("db")
    head_count = lax.axis_size("head")
    groups, slot_count = nbr_row.shape
    tok_rows, local_width = queries.shape
    enc_width = encodings.shape[2]
    slice_len = encodings.shape[1]
    owner_ids = lax.broadcasted_iota(jnp.int32, (1, 1, db_count), 2)
    chosen = nbr_owner[:, :, None] == owner_ids
    wanted = jnp.sum(jnp.where(chosen, nbr_row[:, :, None], 0), axis=1)
    incoming = lax.all_to_all(wanted, "db", split_axis=1, concat_axis=1, tiled=True)
    table = jnp.take(encodings, incoming.T.reshape(-1), axis=0, mode="clip")
    table = table.reshape(db_count, groups * slice_len, enc_width)
    received = lax.all_to_all(table, "db", split_axis=0, concat_axis=0, tiled=True)
    received = received.reshape(db_count * groups, slice_len, enc_width)
    piece = lax.all_gather(grad_out, "head", axis=1, tiled=True)
    d_mixed = lax.dot_general(
        piece, w_out, (((1,), (1,)), ((), ())), preferred_element_type=F32
    ).astype(BF16)
    out_cols = lax.all_to_all(piece, "db", split_axis=1, concat_axis=0, tiled=True)
    picks = nbr_owner * groups + lax.broadcasted_iota(jnp.int32, nbr_owner.shape, 0)
    mine = jnp.take(received, picks.reshape(-1), axis=0, mode="clip")
    slots = lax.all_gather(mine, "head", axis=1, tiled=True)
    slots = slots.reshape(groups, slot_count * slice_len * head_count, enc_width)
    mixed, gwv, gq, gwk = attention_calls(slots, queries, d_mixed, w_key, w_value, nbr_count)
    mixed_all = lax.all_gather(mixed, "db", axis=0, tiled=True)
    out_term = jnp.dot(mixed, w_out, preferred_element_type=F32)
    attended = lax.psum_scatter(out_term.astype(BF16), "head", scatter_dimension=1, tiled=True)
    grad_wo = lax.dot_general(
        mixed_all, out_cols, (((0,), (0,)), ((), ())), preferred_element_type=F32
    )
    grad_wv = lax.psum_scatter(gwv, "db", scatter_dimension=0, tiled=True).astype(F32)
    grad_wk = lax.psum_scatter(gwk, "db", scatter_dimension=0, tiled=True).astype(F32)
    return (attended, gq, grad_wk, grad_wv, grad_wo)


def solution(mesh):
    placed = (
        P("db", "head"),
        P(None, "head"),
        P(None, "head"),
        P("head", None),
        P("db", "head", None),
        P("db", None),
        P("db", None),
        P("db"),
        P("db", "head"),
    )
    return jax.shard_map(
        shards,
        mesh=mesh,
        in_specs=placed,
        out_specs=(
            P("db", "head"),
            P("db", "head"),
            P("db", "head"),
            P("db", "head"),
            P("head", "db"),
        ),
        check_vma=False,
    )
```

```python
import functools
import itertools
import math

import jax
import jax.numpy as jnp
from jax import lax
from jax.experimental import pallas as pl
from jax.experimental.pallas import tpu as pltpu
from jax.sharding import PartitionSpec as P

HD = 128
F32 = jnp.float32
BF16 = jnp.bfloat16
VMEM_LIMIT = 56 * 1024 * 1024


def nt(a, b):
    return lax.dot_general(a, b, (((1,), (1,)), ((), ())), preferred_element_type=F32)


def nn(a, b):
    return jnp.dot(a, b, preferred_element_type=F32)


def tn(a, b):
    return lax.dot_general(a, b, (((0,), (0,)), ((), ())), preferred_element_type=F32)


def forward_kernel(groups, heads, count_ref, slots_ref, q_ref, wk_ref, wv_ref,
                   mixed_ref, probs_ref, pulled_ref):
    tokens = q_ref.shape[0] // groups
    key_len = slots_ref.shape[1]
    tokens_per_slot = key_len // 8
    factor = 1.0 / math.sqrt(HD)
    for c in range(groups):
        rows = slice(c * tokens, (c + 1) * tokens)
        slots = slots_ref[c]
        lifted = jnp.concatenate(
            [
                nt(q_ref[rows, h * HD:(h + 1) * HD], wk_ref[:, h * HD:(h + 1) * HD]).astype(BF16)
                for h in range(heads)
            ],
            axis=0,
        )
        scores = nt(lifted, slots) * factor
        position = lax.broadcasted_iota(jnp.int32, (1, key_len), 1)
        live = position < count_ref[c] * tokens_per_slot
        expo = jnp.where(live, jnp.exp(scores), 0.0)
        probs = (expo / jnp.sum(expo, axis=-1, keepdims=True)).astype(BF16)
        probs_ref[0, c] = probs
        pulled = nn(probs, slots).astype(BF16)
        for h in range(heads):
            part = pulled[h * tokens:(h + 1) * tokens]
            cols = slice(h * HD, (h + 1) * HD)
            mixed_ref[rows, cols] = nn(part, wv_ref[:, cols]).astype(BF16)
            pulled_ref[h, rows, :] = part


def backward_kernel(groups, heads, shares, slots_ref, q_ref, dm_ref, wk_ref, wv_ref, probs_ref,
                    mixing_ref, gq_ref, gwkv_ref, pulled_ref):
    tokens = q_ref.shape[0] // groups
    factor = 1.0 / math.sqrt(HD)
    for c in range(groups):
        rows = slice(c * tokens, (c + 1) * tokens)
        slots = slots_ref[c]
        lifted = jnp.concatenate(
            [
                nt(dm_ref[rows, h * HD:(h + 1) * HD], wv_ref[:, h * HD:(h + 1) * HD]).astype(BF16)
                for h in range(heads)
            ],
            axis=0,
        )
        d_probs = nt(lifted, slots)
        probs = probs_ref[0, c].astype(F32)
        weighted = probs * d_probs
        inner = jnp.sum(weighted, axis=-1, keepdims=True)
        d_scores = ((weighted - probs * inner) * factor).astype(BF16)
        pulled = nn(d_scores, slots).astype(BF16)
        for h in range(heads):
            part = pulled[h * tokens:(h + 1) * tokens]
            cols = slice(h * HD, (h + 1) * HD)
            gq_ref[rows, cols] = nn(part, wk_ref[:, cols]).astype(BF16)
            pulled_ref[h, rows, :] = part
    for h in range(heads):
        cols = slice(h * HD, (h + 1) * HD)
        of_value = tn(mixing_ref[h], dm_ref[:, cols])
        of_key = tn(pulled_ref[h], q_ref[:, cols])
        depth = of_key.shape[0] // shares
        for d in range(shares):
            part = slice(d * depth, (d + 1) * depth)
            both = jnp.concatenate([of_value[part], of_key[part]], axis=0)
            gwkv_ref[d, :, cols] = both.astype(BF16)


def attention_setup(slots, queries):
    groups, key_len, enc = slots.shape
    tok_rows, width = queries.shape
    heads = min(4, width // HD)
    steps = width // (heads * HD)
    part = heads * HD
    group_rows = heads * (tok_rows // groups)
    specs = dict(
        whole=pl.BlockSpec((groups, key_len, enc), lambda i: (0, 0, 0)),
        tok=pl.BlockSpec((tok_rows, part), lambda i: (0, i)),
        weight=pl.BlockSpec((enc, part), lambda i: (0, i)),
        prob=pl.BlockSpec((1, groups, group_rows, key_len), lambda i: (i, 0, 0, 0)),
        pull=pl.BlockSpec((heads, tok_rows, enc), lambda i: (i, 0, 0)),
    )
    shapes = dict(
        tok=jax.ShapeDtypeStruct((tok_rows, width), BF16),
        prob=jax.ShapeDtypeStruct((steps, groups, group_rows, key_len), BF16),
        pull=jax.ShapeDtypeStruct((width // HD, tok_rows, enc), BF16),
    )
    common = dict(
        grid=(steps,),
        compiler_params=pltpu.CompilerParams(vmem_limit_bytes=VMEM_LIMIT),
        cost_estimate=pl.CostEstimate(
            flops=int(4 * groups * group_rows * key_len * enc * steps * 1.2),
            bytes_accessed=20_000_000,
            transcendentals=groups * group_rows * steps * key_len,
        ),
    )
    return groups, heads, specs, shapes, common


def attend(slots, queries, w_key, w_value, nbr_count):
    groups, heads, specs, shapes, common = attention_setup(slots, queries)
    return pl.pallas_call(
        functools.partial(forward_kernel, groups, heads),
        in_specs=[pl.BlockSpec(memory_space=pltpu.SMEM)]
        + [specs[n] for n in ("whole", "tok", "weight", "weight")],
        out_specs=[specs[n] for n in ("tok", "prob", "pull")],
        out_shape=[shapes[n] for n in ("tok", "prob", "pull")],
        **common,
    )(nbr_count, slots, queries, w_key, w_value)


def attend_back(slots, queries, d_mixed, w_key, w_value, probs, mixing, shares):
    groups, heads, specs, shapes, common = attention_setup(slots, queries)
    tok_rows, width = queries.shape
    enc = slots.shape[2]
    rows = 2 * enc // shares
    return pl.pallas_call(
        functools.partial(backward_kernel, groups, heads, shares),
        in_specs=[specs[n] for n in ("whole", "tok", "tok", "weight", "weight", "prob", "pull")],
        out_specs=[
            specs["tok"],
            pl.BlockSpec((shares, rows, heads * HD), lambda i: (0, 0, i)),
        ],
        out_shape=[shapes["tok"], jax.ShapeDtypeStruct((shares, rows, width), BF16)],
        scratch_shapes=[pltpu.VMEM((heads, tok_rows, enc), BF16)],
        **common,
    )(slots, queries, d_mixed, w_key, w_value, probs, mixing)


class Track:
    def __init__(self, me, source, tail, order, buffers, buffer_tail, finish):
        self.me, self.cur, self.tail, self.order = me, source, tail, order
        self.bits = sorted(order, reverse=True)
        self.buffers, self.buffer_tail, self.finish = buffers, buffer_tail, finish
        self.stage = 0
        self.copy = None

    def start(self, send_sem, recv_sem):
        bit = self.order[self.stage]
        mine = lax.rem(self.me // (1 << bit), 2)
        lead = [slice(None)] * len(self.bits)
        lead[self.bits.index(bit)] = 1 - mine
        free = (slice(None),) * (len(self.bits) - 1)
        self.copy = pltpu.make_async_remote_copy(
            src_ref=self.cur.at[tuple(lead) + self.tail],
            dst_ref=self.buffers[self.stage].at[free + self.buffer_tail],
            send_sem=send_sem,
            recv_sem=recv_sem,
            device_id={"db": self.me + (1 - 2 * mine) * (1 << bit)},
            device_id_type=pl.DeviceIdType.MESH,
        )
        self.copy.start()
        return self.copy

    def add(self):
        self.copy.wait_recv()
        bit = self.order[self.stage]
        mine = lax.rem(self.me // (1 << bit), 2)
        place = self.bits.index(bit)
        buffer = self.buffers[self.stage]
        last = self.stage == len(self.order) - 1
        for rest in itertools.product(range(2), repeat=len(self.bits) - 1):
            keep = rest[:place] + (mine,) + rest[place:]
            total = self.cur[keep + self.tail].astype(F32) + buffer[
                rest + self.buffer_tail
            ].astype(F32)
            if last:
                self.finish(total)
            else:
                buffer[rest + self.buffer_tail] = total.astype(BF16)
        self.bits.remove(bit)
        self.cur, self.tail = buffer, self.buffer_tail
        self.stage += 1
        return last


def reduce_kernel(all_bits, low_bits, kv_ref, wo_ref, gv_ref, gk_ref, gwo_ref, *scratch):
    me = lax.axis_index("db")
    kv_bufs = (scratch[0:all_bits], scratch[all_bits:2 * all_bits])
    at = 2 * all_bits
    wo_bufs = (scratch[at:at + low_bits], scratch[at + low_bits:at + 2 * low_bits])
    send_sem, recv_sem = scratch[-2:]

    barrier = pltpu.get_barrier_semaphore()
    for bit in range(all_bits):
        mine = lax.rem(me // (1 << bit), 2)
        pl.semaphore_signal(
            barrier,
            inc=1,
            device_id={"db": me + (1 - 2 * mine) * (1 << bit)},
            device_id_type=pl.DeviceIdType.MESH,
        )
    pl.semaphore_wait(barrier, all_bits)

    depth = gv_ref.shape[0]
    half = kv_ref.shape[-1] // 2
    chunks = min(4, half // 128)
    size = half // chunks
    rows_half = wo_ref.shape[-2] // 2
    wo_size = rows_half // chunks
    rounds = []
    for c in range(chunks):
        pair = []
        for t in range(2):
            order = list(range(all_bits))
            if t == 1:
                order[0], order[1] = order[1], order[0]
            cols = slice(t * half + c * size, t * half + (c + 1) * size)

            def finish(total, cols=cols):
                gv_ref[:, cols] = total[:depth]
                gk_ref[:, cols] = total[depth:]

            pair.append(
                Track(me, kv_ref, (slice(None), cols), order, kv_bufs[t],
                      (slice(None), slice(c * size, (c + 1) * size)), finish)
            )
        rounds.append(pair)
    for c in range(chunks):
        pair = []
        for t in range(2):
            order = list(range(low_bits))
            if t == 1:
                order[0], order[1] = order[1], order[0]
            rows = slice(t * rows_half + c * wo_size, t * rows_half + (c + 1) * wo_size)

            def finish(total, rows=rows):
                gwo_ref[rows, :] = total

            pair.append(
                Track(me, wo_ref, (rows, slice(None)), order, wo_bufs[t],
                      (slice(c * wo_size, (c + 1) * wo_size), slice(None)), finish)
            )
        rounds.append(pair)

    copies = []

    def start(track):
        k = len(copies)
        copies.append(track.start(send_sem.at[k], recv_sem.at[k]))

    for track in rounds[0]:
        start(track)
    active = []
    for t in range(len(rounds) + all_bits):
        if t < len(rounds):
            active.append(rounds[t])
        if t + 1 < len(rounds):
            for track in rounds[t + 1]:
                start(track)
        for pair in list(active):
            for track in pair:
                if track.add():
                    if pair in active:
                        active.remove(pair)
                else:
                    start(track)
    for copy in copies:
        copy.wait_send()


def reduce_scatter(gwkv, gwo):
    shares, rows, width = gwkv.shape
    low, out_rows, out_cols = gwo.shape
    all_bits, low_bits = shares.bit_length() - 1, low.bit_length() - 1
    kv_half, wo_half = width // 2, out_rows // 2
    chunks = min(4, kv_half // 128)
    kv_bufs = [
        pltpu.VMEM((2,) * (all_bits - s - 1) + (rows, kv_half), BF16) for s in range(all_bits)
    ]
    wo_bufs = [
        pltpu.VMEM((2,) * (low_bits - s - 1) + (wo_half, out_cols), BF16) for s in range(low_bits)
    ]
    n_copies = 2 * chunks * (all_bits + low_bits)
    in_vmem = pl.BlockSpec(memory_space=pltpu.VMEM)
    return pl.pallas_call(
        functools.partial(reduce_kernel, all_bits, low_bits),
        in_specs=[in_vmem, in_vmem],
        out_specs=[in_vmem] * 3,
        out_shape=[
            jax.ShapeDtypeStruct((rows // 2, width), F32),
            jax.ShapeDtypeStruct((rows // 2, width), F32),
            jax.ShapeDtypeStruct((out_rows, out_cols), F32),
        ],
        scratch_shapes=kv_bufs + kv_bufs + wo_bufs + wo_bufs
        + [pltpu.SemaphoreType.DMA((n_copies,)), pltpu.SemaphoreType.DMA((n_copies,))],
        compiler_params=pltpu.CompilerParams(
            collective_id=0, has_side_effects=True, vmem_limit_bytes=VMEM_LIMIT
        ),
        cost_estimate=pl.CostEstimate(
            flops=gwkv.size, bytes_accessed=300_000_000, transcendentals=0
        ),
    )(
        gwkv.reshape((2,) * all_bits + (rows, width)),
        gwo.reshape((2,) * low_bits + (out_rows, out_cols)),
    )


def shards(queries, w_key, w_value, w_out, encodings, nbr_row, nbr_owner, nbr_count, grad_out):
    db_count = lax.axis_size("db")
    head_count = lax.axis_size("head")
    groups, slot_count = nbr_row.shape
    tok_rows, local_width = queries.shape
    enc_width = encodings.shape[2]
    slice_len = encodings.shape[1]
    owner_ids = lax.broadcasted_iota(jnp.int32, (1, 1, db_count), 2)
    chosen = nbr_owner[:, :, None] == owner_ids
    wanted = jnp.sum(jnp.where(chosen, nbr_row[:, :, None], 0), axis=1)
    incoming = lax.all_to_all(wanted, "db", split_axis=1, concat_axis=1, tiled=True)
    table = jnp.take(encodings, incoming.T.reshape(-1), axis=0, mode="clip")
    table = table.reshape(db_count, groups * slice_len, enc_width)
    received = lax.all_to_all(table, "db", split_axis=0, concat_axis=0, tiled=True)
    received = received.reshape(db_count * groups, slice_len, enc_width)
    piece = lax.all_gather(grad_out, "head", axis=1, tiled=True)
    d_mixed = lax.dot_general(
        piece, w_out, (((1,), (1,)), ((), ())), preferred_element_type=F32
    ).astype(BF16)
    low = 1 << ((db_count.bit_length() - 1) // 2)
    lines = [list(range(first, db_count, low)) for first in range(low)]
    out_cols = lax.all_to_all(
        piece, "db", split_axis=1, concat_axis=0, axis_index_groups=lines, tiled=True
    )
    picks = nbr_owner * groups + lax.broadcasted_iota(jnp.int32, nbr_owner.shape, 0)
    mine = jnp.take(received, picks.reshape(-1), axis=0, mode="clip")
    slots = lax.all_gather(mine, "head", axis=1, tiled=True)
    slots = slots.reshape(groups, slot_count * slice_len * head_count, enc_width)
    mixed, probs, mixing = attend(slots, queries, w_key, w_value, nbr_count)
    line_mixed = lax.all_gather(mixed, "db", axis=0, axis_index_groups=lines, tiled=True)
    out_term = jnp.dot(mixed, w_out, preferred_element_type=F32)
    attended = lax.psum_scatter(out_term.astype(BF16), "head", scatter_dimension=1, tiled=True)
    gq, gwkv = attend_back(slots, queries, d_mixed, w_key, w_value, probs, mixing, db_count)
    block = out_cols.shape[1] // low
    line_wo = jnp.stack(
        [
            lax.dot_general(
                line_mixed,
                out_cols[:, d * block:(d + 1) * block],
                (((0,), (0,)), ((), ())),
                preferred_element_type=F32,
            ).astype(BF16)
            for d in range(low)
        ]
    )
    grad_wv, grad_wk, grad_wo = reduce_scatter(gwkv, line_wo)
    return (attended, gq, grad_wk, grad_wv, grad_wo)


def solution(mesh):
    placed = (
        P("db", "head"),
        P(None, "head"),
        P(None, "head"),
        P("head", None),
        P("db", "head", None),
        P("db", None),
        P("db", None),
        P("db"),
        P("db", "head"),
    )
    return jax.shard_map(
        shards,
        mesh=mesh,
        in_specs=placed,
        out_specs=(
            P("db", "head"),
            P("db", "head"),
            P("db", "head"),
            P("db", "head"),
            P("head", "db"),
        ),
        check_vma=False,
    )
```

```python
import functools
import itertools
import math

import jax
import jax.numpy as jnp
from jax import lax
from jax.experimental import pallas as pl
from jax.experimental.pallas import tpu as pltpu
from jax.sharding import PartitionSpec as P

HD = 128
F32 = jnp.float32
BF16 = jnp.bfloat16
VMEM_LIMIT = 56 * 1024 * 1024


def nt(a, b):
    return lax.dot_general(a, b, (((1,), (1,)), ((), ())), preferred_element_type=F32)


def nn(a, b):
    return jnp.dot(a, b, preferred_element_type=F32)


def tn(a, b):
    return lax.dot_general(a, b, (((0,), (0,)), ((), ())), preferred_element_type=F32)


def forward_kernel(groups, heads, count_ref, slots_ref, q_ref, wk_ref, wv_ref,
                   mixed_ref, probs_ref, pulled_ref):
    tokens = q_ref.shape[0] // groups
    key_len = slots_ref.shape[1]
    tokens_per_slot = key_len // 8
    factor = 1.0 / math.sqrt(HD)
    for c in range(groups):
        rows = slice(c * tokens, (c + 1) * tokens)
        slots = slots_ref[c]
        lifted = jnp.concatenate(
            [
                nt(q_ref[rows, h * HD:(h + 1) * HD], wk_ref[:, h * HD:(h + 1) * HD]).astype(BF16)
                for h in range(heads)
            ],
            axis=0,
        )
        scores = nt(lifted, slots) * factor
        position = lax.broadcasted_iota(jnp.int32, (1, key_len), 1)
        live = position < count_ref[c] * tokens_per_slot
        expo = jnp.where(live, jnp.exp(scores), 0.0)
        probs = (expo / jnp.sum(expo, axis=-1, keepdims=True)).astype(BF16)
        probs_ref[0, c] = probs
        pulled = nn(probs, slots).astype(BF16)
        for h in range(heads):
            part = pulled[h * tokens:(h + 1) * tokens]
            cols = slice(h * HD, (h + 1) * HD)
            mixed_ref[rows, cols] = nn(part, wv_ref[:, cols]).astype(BF16)
            pulled_ref[h, rows, :] = part


def backward_kernel(groups, heads, shares, slots_ref, q_ref, dm_ref, wk_ref, wv_ref, probs_ref,
                    mixing_ref, gq_ref, gwkv_ref, pulled_ref):
    tokens = q_ref.shape[0] // groups
    factor = 1.0 / math.sqrt(HD)
    for c in range(groups):
        rows = slice(c * tokens, (c + 1) * tokens)
        slots = slots_ref[c]
        lifted = jnp.concatenate(
            [
                nt(dm_ref[rows, h * HD:(h + 1) * HD], wv_ref[:, h * HD:(h + 1) * HD]).astype(BF16)
                for h in range(heads)
            ],
            axis=0,
        )
        d_probs = nt(lifted, slots)
        probs = probs_ref[0, c].astype(F32)
        weighted = probs * d_probs
        inner = jnp.sum(weighted, axis=-1, keepdims=True)
        d_scores = ((weighted - probs * inner) * factor).astype(BF16)
        pulled = nn(d_scores, slots).astype(BF16)
        for h in range(heads):
            part = pulled[h * tokens:(h + 1) * tokens]
            cols = slice(h * HD, (h + 1) * HD)
            gq_ref[rows, cols] = nn(part, wk_ref[:, cols]).astype(BF16)
            pulled_ref[h, rows, :] = part
    for h in range(heads):
        cols = slice(h * HD, (h + 1) * HD)
        of_value = tn(mixing_ref[h], dm_ref[:, cols])
        of_key = tn(pulled_ref[h], q_ref[:, cols])
        depth = of_key.shape[0] // shares
        for d in range(shares):
            part = slice(d * depth, (d + 1) * depth)
            both = jnp.concatenate([of_value[part], of_key[part]], axis=0)
            gwkv_ref[d, :, cols] = both.astype(BF16)


def attention_setup(slots, queries):
    groups, key_len, enc = slots.shape
    tok_rows, width = queries.shape
    heads = min(4, width // HD)
    steps = width // (heads * HD)
    part = heads * HD
    group_rows = heads * (tok_rows // groups)
    specs = dict(
        whole=pl.BlockSpec((groups, key_len, enc), lambda i: (0, 0, 0)),
        tok=pl.BlockSpec((tok_rows, part), lambda i: (0, i)),
        weight=pl.BlockSpec((enc, part), lambda i: (0, i)),
        prob=pl.BlockSpec((1, groups, group_rows, key_len), lambda i: (i, 0, 0, 0)),
        pull=pl.BlockSpec((heads, tok_rows, enc), lambda i: (i, 0, 0)),
    )
    shapes = dict(
        tok=jax.ShapeDtypeStruct((tok_rows, width), BF16),
        prob=jax.ShapeDtypeStruct((steps, groups, group_rows, key_len), BF16),
        pull=jax.ShapeDtypeStruct((width // HD, tok_rows, enc), BF16),
    )
    common = dict(
        grid=(steps,),
        compiler_params=pltpu.CompilerParams(vmem_limit_bytes=VMEM_LIMIT),
        cost_estimate=pl.CostEstimate(
            flops=int(4 * groups * group_rows * key_len * enc * steps * 1.2),
            bytes_accessed=20_000_000,
            transcendentals=groups * group_rows * steps * key_len,
        ),
    )
    return groups, heads, specs, shapes, common


def attend(slots, queries, w_key, w_value, nbr_count):
    groups, heads, specs, shapes, common = attention_setup(slots, queries)
    return pl.pallas_call(
        functools.partial(forward_kernel, groups, heads),
        in_specs=[pl.BlockSpec(memory_space=pltpu.SMEM)]
        + [specs[n] for n in ("whole", "tok", "weight", "weight")],
        out_specs=[specs[n] for n in ("tok", "prob", "pull")],
        out_shape=[shapes[n] for n in ("tok", "prob", "pull")],
        **common,
    )(nbr_count, slots, queries, w_key, w_value)


def attend_back(slots, queries, d_mixed, w_key, w_value, probs, mixing, shares):
    groups, heads, specs, shapes, common = attention_setup(slots, queries)
    tok_rows, width = queries.shape
    enc = slots.shape[2]
    rows = 2 * enc // shares
    return pl.pallas_call(
        functools.partial(backward_kernel, groups, heads, shares),
        in_specs=[specs[n] for n in ("whole", "tok", "tok", "weight", "weight", "prob", "pull")],
        out_specs=[
            specs["tok"],
            pl.BlockSpec((shares, rows, heads * HD), lambda i: (0, 0, i)),
        ],
        out_shape=[shapes["tok"], jax.ShapeDtypeStruct((shares, rows, width), BF16)],
        scratch_shapes=[pltpu.VMEM((heads, tok_rows, enc), BF16)],
        **common,
    )(slots, queries, d_mixed, w_key, w_value, probs, mixing)


class Track:
    def __init__(self, me, source, tail, order, buffers, buffer_tail, finish):
        self.me, self.cur, self.tail, self.order = me, source, tail, order
        self.bits = sorted(order, reverse=True)
        self.buffers, self.buffer_tail, self.finish = buffers, buffer_tail, finish
        self.stage = 0
        self.copy = None

    def start(self, send_sem, recv_sem):
        bit = self.order[self.stage]
        mine = lax.rem(self.me // (1 << bit), 2)
        lead = [slice(None)] * len(self.bits)
        lead[self.bits.index(bit)] = 1 - mine
        free = (slice(None),) * (len(self.bits) - 1)
        self.copy = pltpu.make_async_remote_copy(
            src_ref=self.cur.at[tuple(lead) + self.tail],
            dst_ref=self.buffers[self.stage].at[free + self.buffer_tail],
            send_sem=send_sem,
            recv_sem=recv_sem,
            device_id={"db": self.me + (1 - 2 * mine) * (1 << bit)},
            device_id_type=pl.DeviceIdType.MESH,
        )
        self.copy.start()
        return self.copy

    def add(self):
        self.copy.wait_recv()
        bit = self.order[self.stage]
        mine = lax.rem(self.me // (1 << bit), 2)
        place = self.bits.index(bit)
        buffer = self.buffers[self.stage]
        last = self.stage == len(self.order) - 1
        for rest in itertools.product(range(2), repeat=len(self.bits) - 1):
            keep = rest[:place] + (mine,) + rest[place:]
            total = self.cur[keep + self.tail].astype(F32) + buffer[
                rest + self.buffer_tail
            ].astype(F32)
            if last:
                self.finish(total)
            else:
                buffer[rest + self.buffer_tail] = total.astype(BF16)
        self.bits.remove(bit)
        self.cur, self.tail = buffer, self.buffer_tail
        self.stage += 1
        return last


def reduce_kernel(all_bits, wo_bits, kv_ref, wo_ref, gv_ref, gk_ref, gwo_ref, *scratch):
    me = lax.axis_index("db")
    kv_bufs = (scratch[0:all_bits], scratch[all_bits:2 * all_bits])
    at = 2 * all_bits
    wo_bufs = (scratch[at:at + wo_bits], scratch[at + wo_bits:at + 2 * wo_bits])
    send_sem, recv_sem = scratch[-2:]

    barrier = pltpu.get_barrier_semaphore()
    for bit in range(all_bits):
        mine = lax.rem(me // (1 << bit), 2)
        pl.semaphore_signal(
            barrier,
            inc=1,
            device_id={"db": me + (1 - 2 * mine) * (1 << bit)},
            device_id_type=pl.DeviceIdType.MESH,
        )
    pl.semaphore_wait(barrier, all_bits)

    depth = gv_ref.shape[0]
    half = kv_ref.shape[-1] // 2
    chunks = min(4, half // 128)
    size = half // chunks
    rows_half = wo_ref.shape[-2] // 2
    wo_size = rows_half // chunks
    rounds = []
    for c in range(chunks):
        pair = []
        rounds.append(pair)
        for t in range(2):
            order = list(range(all_bits))
            if t == 1:
                order[0], order[1] = order[1], order[0]
            cols = slice(t * half + c * size, t * half + (c + 1) * size)

            def finish(total, cols=cols):
                gv_ref[:, cols] = total[:depth]
                gk_ref[:, cols] = total[depth:]

            pair.append(
                Track(me, kv_ref, (slice(None), cols), order, kv_bufs[t],
                      (slice(None), slice(c * size, (c + 1) * size)), finish)
            )
        pair = []
        rounds.append(pair)
        for t in range(2):
            order = list(range(all_bits - wo_bits, all_bits))
            rows = slice(t * rows_half + c * wo_size, t * rows_half + (c + 1) * wo_size)

            def finish(total, rows=rows):
                gwo_ref[rows, :] = total

            pair.append(
                Track(me, wo_ref, (rows, slice(None)), order, wo_bufs[t],
                      (slice(c * wo_size, (c + 1) * wo_size), slice(None)), finish)
            )

    copies = []

    def start(track):
        k = len(copies)
        copies.append(track.start(send_sem.at[k], recv_sem.at[k]))

    for track in rounds[0]:
        start(track)
    active = []
    for t in range(len(rounds) + all_bits):
        if t < len(rounds):
            active.append(rounds[t])
        if t + 1 < len(rounds):
            for track in rounds[t + 1]:
                start(track)
        for pair in list(active):
            for track in pair:
                if track.add():
                    if pair in active:
                        active.remove(pair)
                else:
                    start(track)
    for copy in copies:
        copy.wait_send()


def reduce_scatter(gwkv, gwo):
    shares, rows, width = gwkv.shape
    low, out_rows, out_cols = gwo.shape
    all_bits, wo_bits = shares.bit_length() - 1, low.bit_length() - 1
    kv_half, wo_half = width // 2, out_rows // 2
    chunks = min(4, kv_half // 128)
    kv_bufs = [
        pltpu.VMEM((2,) * (all_bits - s - 1) + (rows, kv_half), BF16) for s in range(all_bits)
    ]
    wo_bufs = [
        pltpu.VMEM((2,) * (wo_bits - s - 1) + (wo_half, out_cols), BF16) for s in range(wo_bits)
    ]
    n_copies = 2 * chunks * (all_bits + wo_bits)
    in_vmem = pl.BlockSpec(memory_space=pltpu.VMEM)
    return pl.pallas_call(
        functools.partial(reduce_kernel, all_bits, wo_bits),
        in_specs=[in_vmem, in_vmem],
        out_specs=[in_vmem] * 3,
        out_shape=[
            jax.ShapeDtypeStruct((rows // 2, width), F32),
            jax.ShapeDtypeStruct((rows // 2, width), F32),
            jax.ShapeDtypeStruct((out_rows, out_cols), F32),
        ],
        scratch_shapes=kv_bufs + kv_bufs + wo_bufs + wo_bufs
        + [pltpu.SemaphoreType.DMA((n_copies,)), pltpu.SemaphoreType.DMA((n_copies,))],
        compiler_params=pltpu.CompilerParams(
            collective_id=0, has_side_effects=True, vmem_limit_bytes=VMEM_LIMIT
        ),
        cost_estimate=pl.CostEstimate(
            flops=gwkv.size, bytes_accessed=300_000_000, transcendentals=0
        ),
    )(
        gwkv.reshape((2,) * all_bits + (rows, width)),
        gwo.reshape((2,) * wo_bits + (out_rows, out_cols)),
    )


def remote(source, target, send_sem, recv_sem, device):
    copy = pltpu.make_async_remote_copy(
        src_ref=source,
        dst_ref=target,
        send_sem=send_sem,
        recv_sem=recv_sem,
        device_id=device,
        device_id_type=pl.DeviceIdType.MESH,
    )
    copy.start()
    return copy


def exchange_kernel(low, wanted_ref, grad_ref, incoming_ref, piece_ref, cols_ref,
                    send_sem, recv_sem):
    db_count, head_count = lax.axis_size("db"), lax.axis_size("head")
    me, head = lax.axis_index("db"), lax.axis_index("head")
    tokens, width = grad_ref.shape
    high = db_count // low
    block = width * head_count // db_count
    lower, upper = lax.rem(me, low), me // low
    barrier = pltpu.get_barrier_semaphore()
    for k in range(1, db_count):
        pl.semaphore_signal(barrier, inc=1, device_id={"db": lax.rem(me + k, db_count)},
                            device_id_type=pl.DeviceIdType.MESH)
    for k in range(1, head_count):
        pl.semaphore_signal(barrier, inc=1, device_id={"head": lax.rem(head + k, head_count)},
                            device_id_type=pl.DeviceIdType.MESH)
    pl.semaphore_wait(barrier, db_count + head_count - 2)
    copies = []
    own = pl.ds(pl.multiple_of(head * width, width), width)
    for k in range(1, head_count):
        n = len(copies)
        copies.append(remote(grad_ref, piece_ref.at[:, own], send_sem.at[n], recv_sem.at[n],
                             {"head": lax.rem(head + k, head_count)}))
    for k in range(1, db_count):
        n = len(copies)
        to = lax.rem(me + k, db_count)
        copies.append(remote(wanted_ref.at[to], incoming_ref.at[me], send_sem.at[n],
                             recv_sem.at[n], {"db": to}))
    piece_ref[:, own] = grad_ref[...]
    incoming_ref[me] = wanted_ref[me]
    for copy in copies[:head_count - 1]:
        copy.wait_recv()
    rows = pl.ds(pl.multiple_of(lower * tokens, tokens), tokens)
    for k in range(1, low):
        to = lax.rem(lower + k, low)
        for u in range(high):
            n = len(copies)
            cols = pl.ds(pl.multiple_of((u * low + to) * block, block), block)
            copies.append(remote(piece_ref.at[:, cols],
                                 cols_ref.at[rows, u * block:(u + 1) * block],
                                 send_sem.at[n], recv_sem.at[n], {"db": upper * low + to}))
    for u in range(high):
        cols = pl.ds(pl.multiple_of((u * low + lower) * block, block), block)
        cols_ref[rows, u * block:(u + 1) * block] = piece_ref[:, cols]
    for copy in copies[head_count - 1:]:
        copy.wait_recv()
    for copy in copies:
        copy.wait_send()


def exchange(wanted, grad_out, low):
    db_count, head_count = lax.axis_size("db"), lax.axis_size("head")
    tokens, width = grad_out.shape
    full = width * head_count
    n = head_count - 1 + db_count - 1 + (low - 1) * (db_count // low)
    in_vmem = pl.BlockSpec(memory_space=pltpu.VMEM)
    return pl.pallas_call(
        functools.partial(exchange_kernel, low),
        in_specs=[in_vmem] * 2,
        out_specs=[in_vmem] * 3,
        out_shape=[
            jax.ShapeDtypeStruct(wanted.shape, jnp.int32),
            jax.ShapeDtypeStruct((tokens, full), BF16),
            jax.ShapeDtypeStruct((low * tokens, full // low), BF16),
        ],
        scratch_shapes=[pltpu.SemaphoreType.DMA((n,)), pltpu.SemaphoreType.DMA((n,))],
        compiler_params=pltpu.CompilerParams(
            collective_id=1, has_side_effects=True, vmem_limit_bytes=VMEM_LIMIT
        ),
    )(wanted, grad_out)


def share_kernel(mine_ref, whole_ref, send_sem, recv_sem, local_sem):
    head_count, head = lax.axis_size("head"), lax.axis_index("head")
    depth = mine_ref.shape[1]
    barrier = pltpu.get_barrier_semaphore()
    for k in range(1, head_count):
        pl.semaphore_signal(barrier, inc=1, device_id={"head": lax.rem(head + k, head_count)},
                            device_id_type=pl.DeviceIdType.MESH)
    pl.semaphore_wait(barrier, head_count - 1)
    place = whole_ref.at[:, pl.ds(pl.multiple_of(head * depth, depth), depth), :]
    copies = [
        remote(mine_ref, place, send_sem.at[k - 1], recv_sem.at[k - 1],
               {"head": lax.rem(head + k, head_count)})
        for k in range(1, head_count)
    ]
    local = pltpu.make_async_copy(mine_ref, place, local_sem)
    local.start()
    for copy in copies:
        copy.wait()
    local.wait()


def share(mine):
    head_count = lax.axis_size("head")
    rows, depth, enc = mine.shape
    in_vmem = pl.BlockSpec(memory_space=pltpu.VMEM)
    return pl.pallas_call(
        share_kernel,
        in_specs=[in_vmem],
        out_specs=in_vmem,
        out_shape=jax.ShapeDtypeStruct((rows, depth * head_count, enc), BF16),
        scratch_shapes=[
            pltpu.SemaphoreType.DMA((head_count - 1,)),
            pltpu.SemaphoreType.DMA((head_count - 1,)),
            pltpu.SemaphoreType.DMA,
        ],
        compiler_params=pltpu.CompilerParams(
            collective_id=2, has_side_effects=True, vmem_limit_bytes=VMEM_LIMIT
        ),
    )(mine)


def shards(queries, w_key, w_value, w_out, encodings, nbr_row, nbr_owner, nbr_count, grad_out):
    db_count = lax.axis_size("db")
    head_count = lax.axis_size("head")
    groups, slot_count = nbr_row.shape
    tok_rows, local_width = queries.shape
    enc_width = encodings.shape[2]
    slice_len = encodings.shape[1]
    owner_ids = lax.broadcasted_iota(jnp.int32, (1, 1, db_count), 2)
    chosen = nbr_owner[:, :, None] == owner_ids
    wanted = jnp.sum(jnp.where(chosen, nbr_row[:, :, None], 0), axis=1)
    low = 1 << ((db_count.bit_length() - 1) // 2)
    planes = [list(range(first, first + low)) for first in range(0, db_count, low)]
    padded = jnp.broadcast_to(
        jnp.pad(wanted.T, ((0, 0), (0, 128 - groups)))[:, None, :], (db_count, 8, 128)
    )
    incoming, piece, out_cols = exchange(padded, grad_out, low)
    table = jnp.take(encodings, incoming[:, 0, :groups].reshape(-1), axis=0, mode="clip")
    table = table.reshape(db_count, groups * slice_len, enc_width)
    received = lax.all_to_all(table, "db", split_axis=0, concat_axis=0, tiled=True)
    d_mixed = lax.dot_general(
        piece, w_out, (((1,), (1,)), ((), ())), preferred_element_type=F32
    ).astype(BF16)
    received, d_mixed = lax.optimization_barrier((received, d_mixed))
    received = received.reshape(db_count * groups, slice_len, enc_width)
    picks = nbr_owner * groups + lax.broadcasted_iota(jnp.int32, nbr_owner.shape, 0)
    mine = jnp.take(received, picks.reshape(-1), axis=0, mode="clip")
    slots = share(mine).reshape(groups, slot_count * slice_len * head_count, enc_width)
    mixed, probs, mixing = attend(slots, queries, w_key, w_value, nbr_count)
    plane_mixed = lax.all_gather(mixed, "db", axis=0, axis_index_groups=planes, tiled=True)
    out_term = jnp.dot(mixed, w_out, preferred_element_type=F32)
    attended = lax.psum_scatter(out_term.astype(BF16), "head", scatter_dimension=1, tiled=True)
    gq, gwkv = attend_back(slots, queries, d_mixed, w_key, w_value, probs, mixing, db_count)
    high = db_count // low
    block = out_cols.shape[1] // high
    plane_wo = jnp.stack(
        [
            lax.dot_general(
                plane_mixed,
                out_cols[:, d * block:(d + 1) * block],
                (((0,), (0,)), ((), ())),
                preferred_element_type=F32,
            ).astype(BF16)
            for d in range(high)
        ]
    )
    grad_wv, grad_wk, grad_wo = reduce_scatter(gwkv, plane_wo)
    return (attended, gq, grad_wk, grad_wv, grad_wo)


def solution(mesh):
    placed = (
        P("db", "head"),
        P(None, "head"),
        P(None, "head"),
        P("head", None),
        P("db", "head", None),
        P("db", None),
        P("db", None),
        P("db"),
        P("db", "head"),
    )
    return jax.shard_map(
        shards,
        mesh=mesh,
        in_specs=placed,
        out_specs=(
            P("db", "head"),
            P("db", "head"),
            P("db", "head"),
            P("db", "head"),
            P("head", "db"),
        ),
        check_vma=False,
    )
```

```python
import functools
import itertools
import math

import jax
import jax.numpy as jnp
from jax import lax
from jax.experimental import pallas as pl
from jax.experimental.pallas import tpu as pltpu
from jax.sharding import PartitionSpec as P

HD = 128
F32 = jnp.float32
BF16 = jnp.bfloat16
VMEM_LIMIT = 56 * 1024 * 1024


def nt(a, b):
    return lax.dot_general(a, b, (((1,), (1,)), ((), ())), preferred_element_type=F32)


def nn(a, b):
    return jnp.dot(a, b, preferred_element_type=F32)


def tn(a, b):
    return lax.dot_general(a, b, (((0,), (0,)), ((), ())), preferred_element_type=F32)


def forward_kernel(groups, heads, count_ref, slots_ref, q_ref, wk_ref, wv_ref,
                   mixed_ref, probs_ref, pulled_ref):
    tokens = q_ref.shape[0] // groups
    key_len = slots_ref.shape[1]
    tokens_per_slot = key_len // 8
    factor = 1.0 / math.sqrt(HD)
    for c in range(groups):
        rows = slice(c * tokens, (c + 1) * tokens)
        slots = slots_ref[c]
        lifted = jnp.concatenate(
            [
                nt(q_ref[rows, h * HD:(h + 1) * HD], wk_ref[:, h * HD:(h + 1) * HD]).astype(BF16)
                for h in range(heads)
            ],
            axis=0,
        )
        scores = nt(lifted, slots) * factor
        position = lax.broadcasted_iota(jnp.int32, (1, key_len), 1)
        live = position < count_ref[c] * tokens_per_slot
        expo = jnp.where(live, jnp.exp(scores), 0.0)
        probs = (expo / jnp.sum(expo, axis=-1, keepdims=True)).astype(BF16)
        probs_ref[0, c] = probs
        pulled = nn(probs, slots).astype(BF16)
        for h in range(heads):
            part = pulled[h * tokens:(h + 1) * tokens]
            cols = slice(h * HD, (h + 1) * HD)
            mixed_ref[rows, cols] = nn(part, wv_ref[:, cols]).astype(BF16)
            pulled_ref[h, rows, :] = part


def backward_kernel(groups, heads, shares, slots_ref, q_ref, dm_ref, wk_ref, wv_ref, probs_ref,
                    mixing_ref, gq_ref, gwkv_ref, pulled_ref):
    tokens = q_ref.shape[0] // groups
    factor = 1.0 / math.sqrt(HD)
    for c in range(groups):
        rows = slice(c * tokens, (c + 1) * tokens)
        slots = slots_ref[c]
        lifted = jnp.concatenate(
            [
                nt(dm_ref[rows, h * HD:(h + 1) * HD], wv_ref[:, h * HD:(h + 1) * HD]).astype(BF16)
                for h in range(heads)
            ],
            axis=0,
        )
        d_probs = nt(lifted, slots)
        probs = probs_ref[0, c].astype(F32)
        weighted = probs * d_probs
        inner = jnp.sum(weighted, axis=-1, keepdims=True)
        d_scores = ((weighted - probs * inner) * factor).astype(BF16)
        pulled = nn(d_scores, slots).astype(BF16)
        for h in range(heads):
            part = pulled[h * tokens:(h + 1) * tokens]
            cols = slice(h * HD, (h + 1) * HD)
            gq_ref[rows, cols] = nn(part, wk_ref[:, cols]).astype(BF16)
            pulled_ref[h, rows, :] = part
    for h in range(heads):
        cols = slice(h * HD, (h + 1) * HD)
        of_value = tn(mixing_ref[h], dm_ref[:, cols])
        of_key = tn(pulled_ref[h], q_ref[:, cols])
        depth = of_key.shape[0] // shares
        for d in range(shares):
            part = slice(d * depth, (d + 1) * depth)
            both = jnp.concatenate([of_value[part], of_key[part]], axis=0)
            gwkv_ref[d, :, cols] = both.astype(BF16)


def attention_setup(slots, queries):
    groups, key_len, enc = slots.shape
    tok_rows, width = queries.shape
    heads = min(4, width // HD)
    steps = width // (heads * HD)
    part = heads * HD
    group_rows = heads * (tok_rows // groups)
    specs = dict(
        whole=pl.BlockSpec((groups, key_len, enc), lambda i: (0, 0, 0)),
        tok=pl.BlockSpec((tok_rows, part), lambda i: (0, i)),
        weight=pl.BlockSpec((enc, part), lambda i: (0, i)),
        prob=pl.BlockSpec((1, groups, group_rows, key_len), lambda i: (i, 0, 0, 0)),
        pull=pl.BlockSpec((heads, tok_rows, enc), lambda i: (i, 0, 0)),
    )
    shapes = dict(
        tok=jax.ShapeDtypeStruct((tok_rows, width), BF16),
        prob=jax.ShapeDtypeStruct((steps, groups, group_rows, key_len), BF16),
        pull=jax.ShapeDtypeStruct((width // HD, tok_rows, enc), BF16),
    )
    common = dict(
        grid=(steps,),
        compiler_params=pltpu.CompilerParams(vmem_limit_bytes=VMEM_LIMIT),
        cost_estimate=pl.CostEstimate(
            flops=int(4 * groups * group_rows * key_len * enc * steps * 1.2),
            bytes_accessed=20_000_000,
            transcendentals=groups * group_rows * steps * key_len,
        ),
    )
    return groups, heads, specs, shapes, common


def attend(slots, queries, w_key, w_value, nbr_count):
    groups, heads, specs, shapes, common = attention_setup(slots, queries)
    return pl.pallas_call(
        functools.partial(forward_kernel, groups, heads),
        in_specs=[pl.BlockSpec(memory_space=pltpu.SMEM)]
        + [specs[n] for n in ("whole", "tok", "weight", "weight")],
        out_specs=[specs[n] for n in ("tok", "prob", "pull")],
        out_shape=[shapes[n] for n in ("tok", "prob", "pull")],
        **common,
    )(nbr_count, slots, queries, w_key, w_value)


def attend_back(slots, queries, d_mixed, w_key, w_value, probs, mixing, shares):
    groups, heads, specs, shapes, common = attention_setup(slots, queries)
    tok_rows, width = queries.shape
    enc = slots.shape[2]
    rows = 2 * enc // shares
    return pl.pallas_call(
        functools.partial(backward_kernel, groups, heads, shares),
        in_specs=[specs[n] for n in ("whole", "tok", "tok", "weight", "weight", "prob", "pull")],
        out_specs=[
            specs["tok"],
            pl.BlockSpec((shares, rows, heads * HD), lambda i: (0, 0, i)),
        ],
        out_shape=[shapes["tok"], jax.ShapeDtypeStruct((shares, rows, width), BF16)],
        scratch_shapes=[pltpu.VMEM((heads, tok_rows, enc), BF16)],
        **common,
    )(slots, queries, d_mixed, w_key, w_value, probs, mixing)


class Track:
    def __init__(self, me, source, tail, order, buffers, buffer_tail, finish):
        self.me, self.cur, self.tail, self.order = me, source, tail, order
        self.bits = sorted(order, reverse=True)
        self.buffers, self.buffer_tail, self.finish = buffers, buffer_tail, finish
        self.stage = 0
        self.copy = None

    def start(self, send_sem, recv_sem):
        bit = self.order[self.stage]
        mine = lax.rem(self.me // (1 << bit), 2)
        lead = [slice(None)] * len(self.bits)
        lead[self.bits.index(bit)] = 1 - mine
        free = (slice(None),) * (len(self.bits) - 1)
        self.copy = pltpu.make_async_remote_copy(
            src_ref=self.cur.at[tuple(lead) + self.tail],
            dst_ref=self.buffers[self.stage].at[free + self.buffer_tail],
            send_sem=send_sem,
            recv_sem=recv_sem,
            device_id={"db": self.me + (1 - 2 * mine) * (1 << bit)},
            device_id_type=pl.DeviceIdType.MESH,
        )
        self.copy.start()
        return self.copy

    def add(self):
        self.copy.wait_recv()
        bit = self.order[self.stage]
        mine = lax.rem(self.me // (1 << bit), 2)
        place = self.bits.index(bit)
        buffer = self.buffers[self.stage]
        last = self.stage == len(self.order) - 1
        for rest in itertools.product(range(2), repeat=len(self.bits) - 1):
            keep = rest[:place] + (mine,) + rest[place:]
            total = self.cur[keep + self.tail].astype(F32) + buffer[
                rest + self.buffer_tail
            ].astype(F32)
            if last:
                self.finish(total)
            else:
                buffer[rest + self.buffer_tail] = total.astype(BF16)
        self.bits.remove(bit)
        self.cur, self.tail = buffer, self.buffer_tail
        self.stage += 1
        return last


def reduce_kernel(all_bits, wo_bits, kv_ref, wo_ref, gv_ref, gk_ref, gwo_ref, *scratch):
    me = lax.axis_index("db")
    kv_bufs = (scratch[0:all_bits], scratch[all_bits:2 * all_bits])
    at = 2 * all_bits
    wo_bufs = (scratch[at:at + wo_bits], scratch[at + wo_bits:at + 2 * wo_bits])
    send_sem, recv_sem = scratch[-2:]

    barrier = pltpu.get_barrier_semaphore()
    for bit in range(all_bits):
        mine = lax.rem(me // (1 << bit), 2)
        pl.semaphore_signal(
            barrier,
            inc=1,
            device_id={"db": me + (1 - 2 * mine) * (1 << bit)},
            device_id_type=pl.DeviceIdType.MESH,
        )
    pl.semaphore_wait(barrier, all_bits)

    depth = gv_ref.shape[0]
    half = kv_ref.shape[-1] // 2
    chunks = min(4, half // 128)
    size = half // chunks
    rows_half = wo_ref.shape[-2] // 2
    wo_size = rows_half // chunks
    rounds = []
    for c in range(chunks):
        pair = []
        rounds.append(pair)
        for t in range(2):
            order = list(range(all_bits))
            if t == 1:
                order[0], order[1] = order[1], order[0]
            cols = slice(t * half + c * size, t * half + (c + 1) * size)

            def finish(total, cols=cols):
                gv_ref[:, cols] = total[:depth]
                gk_ref[:, cols] = total[depth:]

            pair.append(
                Track(me, kv_ref, (slice(None), cols), order, kv_bufs[t],
                      (slice(None), slice(c * size, (c + 1) * size)), finish)
            )
        pair = []
        rounds.append(pair)
        for t in range(2):
            order = list(range(all_bits - wo_bits, all_bits))
            rows = slice(t * rows_half + c * wo_size, t * rows_half + (c + 1) * wo_size)

            def finish(total, rows=rows):
                gwo_ref[rows, :] = total

            pair.append(
                Track(me, wo_ref, (rows, slice(None)), order, wo_bufs[t],
                      (slice(c * wo_size, (c + 1) * wo_size), slice(None)), finish)
            )

    copies = []

    def start(track):
        k = len(copies)
        copies.append(track.start(send_sem.at[k], recv_sem.at[k]))

    for pair in rounds[0:2] + rounds[3::2] + rounds[2:3]:
        for track in pair:
            start(track)
    active = []
    for t in range(len(rounds) + all_bits):
        active += rounds[t:t + 1]
        if t % 2 == 0 and t + 4 < len(rounds):
            for track in rounds[t + 4]:
                start(track)
        for pair in list(active):
            for track in pair:
                if not track.add():
                    start(track)
                elif pair in active:
                    active.remove(pair)
    for copy in copies:
        copy.wait_send()


def reduce_scatter(gwkv, gwo):
    shares, rows, width = gwkv.shape
    low, out_rows, out_cols = gwo.shape
    all_bits, wo_bits = shares.bit_length() - 1, low.bit_length() - 1
    kv_half, wo_half = width // 2, out_rows // 2
    chunks = min(4, kv_half // 128)
    kv_bufs = [
        pltpu.VMEM((2,) * (all_bits - s - 1) + (rows, kv_half), BF16) for s in range(all_bits)
    ]
    wo_bufs = [
        pltpu.VMEM((2,) * (wo_bits - s - 1) + (wo_half, out_cols), BF16) for s in range(wo_bits)
    ]
    n_copies = 2 * chunks * (all_bits + wo_bits)
    in_vmem = pl.BlockSpec(memory_space=pltpu.VMEM)
    return pl.pallas_call(
        functools.partial(reduce_kernel, all_bits, wo_bits),
        in_specs=[in_vmem, in_vmem],
        out_specs=[in_vmem] * 3,
        out_shape=[
            jax.ShapeDtypeStruct((rows // 2, width), F32),
            jax.ShapeDtypeStruct((rows // 2, width), F32),
            jax.ShapeDtypeStruct((out_rows, out_cols), F32),
        ],
        scratch_shapes=kv_bufs + kv_bufs + wo_bufs + wo_bufs
        + [pltpu.SemaphoreType.DMA((n_copies,)), pltpu.SemaphoreType.DMA((n_copies,))],
        compiler_params=pltpu.CompilerParams(
            collective_id=0, has_side_effects=True, vmem_limit_bytes=VMEM_LIMIT
        ),
        cost_estimate=pl.CostEstimate(
            flops=gwkv.size, bytes_accessed=300_000_000, transcendentals=0
        ),
    )(
        gwkv.reshape((2,) * all_bits + (rows, width)),
        gwo.reshape((2,) * wo_bits + (out_rows, out_cols)),
    )


def remote(source, target, send_sem, recv_sem, device):
    copy = pltpu.make_async_remote_copy(
        src_ref=source,
        dst_ref=target,
        send_sem=send_sem,
        recv_sem=recv_sem,
        device_id=device,
        device_id_type=pl.DeviceIdType.MESH,
    )
    copy.start()
    return copy


def greet(db_peers, head_peers):
    barrier = pltpu.get_barrier_semaphore()
    for device in [{"db": d} for d in db_peers] + [{"head": h} for h in head_peers]:
        pl.semaphore_signal(barrier, inc=1, device_id=device,
                            device_id_type=pl.DeviceIdType.MESH)
    pl.semaphore_wait(barrier, len(db_peers) + len(head_peers))


def request_kernel(wanted_ref, incoming_ref, send_sem, recv_sem):
    db_count, me = lax.axis_size("db"), lax.axis_index("db")
    peers = [lax.rem(me + k, db_count) for k in range(1, db_count)]
    greet(peers, [])
    copies = [
        remote(wanted_ref.at[to], incoming_ref.at[me], send_sem.at[n], recv_sem.at[n], {"db": to})
        for n, to in enumerate(peers)
    ]
    incoming_ref[me] = wanted_ref[me]
    for copy in copies:
        copy.wait()


def exchange_kernel(low, grad_ref, piece_ref, cols_ref, send_sem, recv_sem):
    db_count, head_count = lax.axis_size("db"), lax.axis_size("head")
    me, head = lax.axis_index("db"), lax.axis_index("head")
    tokens, width = grad_ref.shape
    high = db_count // low
    block = width * head_count // db_count
    lower, upper = lax.rem(me, low), me // low
    near = [lax.rem(lower + k, low) for k in range(1, low)]
    heads = [lax.rem(head + k, head_count) for k in range(1, head_count)]
    greet([upper * low + to for to in near], heads)
    copies = []
    own = pl.ds(pl.multiple_of(head * width, width), width)
    for to in heads:
        n = len(copies)
        copies.append(remote(grad_ref, piece_ref.at[:, own], send_sem.at[n], recv_sem.at[n],
                             {"head": to}))
    piece_ref[:, own] = grad_ref[...]
    for copy in copies:
        copy.wait_recv()
    rows = pl.ds(pl.multiple_of(lower * tokens, tokens), tokens)
    for to in near:
        for u in range(high):
            n = len(copies)
            cols = pl.ds(pl.multiple_of((u * low + to) * block, block), block)
            copies.append(remote(piece_ref.at[:, cols],
                                 cols_ref.at[rows, u * block:(u + 1) * block],
                                 send_sem.at[n], recv_sem.at[n], {"db": upper * low + to}))
    for u in range(high):
        cols = pl.ds(pl.multiple_of((u * low + lower) * block, block), block)
        cols_ref[rows, u * block:(u + 1) * block] = piece_ref[:, cols]
    for copy in copies[head_count - 1:]:
        copy.wait_recv()
    for copy in copies:
        copy.wait_send()


def request(wanted):
    n = lax.axis_size("db") - 1
    in_vmem = pl.BlockSpec(memory_space=pltpu.VMEM)
    return pl.pallas_call(
        request_kernel,
        in_specs=[in_vmem],
        out_specs=in_vmem,
        out_shape=jax.ShapeDtypeStruct(wanted.shape, jnp.int32),
        scratch_shapes=[pltpu.SemaphoreType.DMA((n,)), pltpu.SemaphoreType.DMA((n,))],
        compiler_params=pltpu.CompilerParams(collective_id=3, has_side_effects=True),
    )(wanted)


def exchange(grad_out, low):
    db_count, head_count = lax.axis_size("db"), lax.axis_size("head")
    tokens, width = grad_out.shape
    full = width * head_count
    n = head_count - 1 + (low - 1) * (db_count // low)
    in_vmem = pl.BlockSpec(memory_space=pltpu.VMEM)
    return pl.pallas_call(
        functools.partial(exchange_kernel, low),
        in_specs=[in_vmem],
        out_specs=[in_vmem] * 2,
        out_shape=[
            jax.ShapeDtypeStruct((tokens, full), BF16),
            jax.ShapeDtypeStruct((low * tokens, full // low), BF16),
        ],
        scratch_shapes=[pltpu.SemaphoreType.DMA((n,)), pltpu.SemaphoreType.DMA((n,))],
        compiler_params=pltpu.CompilerParams(
            collective_id=1, has_side_effects=True, vmem_limit_bytes=VMEM_LIMIT
        ),
        cost_estimate=pl.CostEstimate(flops=0, bytes_accessed=40_000_000, transcendentals=0),
    )(grad_out)


def share_kernel(mine_ref, whole_ref, send_sem, recv_sem, local_sem):
    head_count, head = lax.axis_size("head"), lax.axis_index("head")
    depth = mine_ref.shape[1]
    barrier = pltpu.get_barrier_semaphore()
    for k in range(1, head_count):
        pl.semaphore_signal(barrier, inc=1, device_id={"head": lax.rem(head + k, head_count)},
                            device_id_type=pl.DeviceIdType.MESH)
    pl.semaphore_wait(barrier, head_count - 1)
    place = whole_ref.at[:, pl.ds(pl.multiple_of(head * depth, depth), depth), :]
    copies = [
        remote(mine_ref, place, send_sem.at[k - 1], recv_sem.at[k - 1],
               {"head": lax.rem(head + k, head_count)})
        for k in range(1, head_count)
    ]
    local = pltpu.make_async_copy(mine_ref, place, local_sem)
    local.start()
    for copy in copies:
        copy.wait()
    local.wait()


def share(mine):
    head_count = lax.axis_size("head")
    rows, depth, enc = mine.shape
    in_vmem = pl.BlockSpec(memory_space=pltpu.VMEM)
    return pl.pallas_call(
        share_kernel,
        in_specs=[in_vmem],
        out_specs=in_vmem,
        out_shape=jax.ShapeDtypeStruct((rows, depth * head_count, enc), BF16),
        scratch_shapes=[
            pltpu.SemaphoreType.DMA((head_count - 1,)),
            pltpu.SemaphoreType.DMA((head_count - 1,)),
            pltpu.SemaphoreType.DMA,
        ],
        compiler_params=pltpu.CompilerParams(
            collective_id=2, has_side_effects=True, vmem_limit_bytes=VMEM_LIMIT
        ),
    )(mine)


def shards(queries, w_key, w_value, w_out, encodings, nbr_row, nbr_owner, nbr_count, grad_out):
    db_count = lax.axis_size("db")
    head_count = lax.axis_size("head")
    groups, slot_count = nbr_row.shape
    tok_rows, local_width = queries.shape
    enc_width = encodings.shape[2]
    slice_len = encodings.shape[1]
    owner_ids = lax.broadcasted_iota(jnp.int32, (1, 1, db_count), 2)
    chosen = nbr_owner[:, :, None] == owner_ids
    wanted = jnp.sum(jnp.where(chosen, nbr_row[:, :, None], 0), axis=1)
    low = 1 << ((db_count.bit_length() - 1) // 2)
    planes = [list(range(first, first + low)) for first in range(0, db_count, low)]
    padded = jnp.broadcast_to(
        jnp.pad(wanted.T, ((0, 0), (0, 128 - groups)))[:, None, :], (db_count, 8, 128)
    )
    incoming = request(padded)
    table = jnp.take(encodings, incoming[:, 0, :groups].reshape(-1), axis=0, mode="clip")
    table = table.reshape(db_count, groups * slice_len, enc_width)
    received = lax.all_to_all(table, "db", split_axis=0, concat_axis=0, tiled=True)
    piece, out_cols = exchange(lax.optimization_barrier((grad_out, table))[0], low)
    d_mixed = lax.dot_general(
        piece, w_out, (((1,), (1,)), ((), ())), preferred_element_type=F32
    ).astype(BF16)
    received, d_mixed, out_cols = lax.optimization_barrier((received, d_mixed, out_cols))
    received = received.reshape(db_count * groups, slice_len, enc_width)
    picks = nbr_owner * groups + lax.broadcasted_iota(jnp.int32, nbr_owner.shape, 0)
    mine = jnp.take(received, picks.reshape(-1), axis=0, mode="clip")
    slots = share(mine).reshape(groups, slot_count * slice_len * head_count, enc_width)
    mixed, probs, mixing = attend(slots, queries, w_key, w_value, nbr_count)
    plane_mixed = lax.all_gather(mixed, "db", axis=0, axis_index_groups=planes, tiled=True)
    out_term = jnp.dot(mixed, w_out, preferred_element_type=F32)
    attended = lax.psum_scatter(out_term.astype(BF16), "head", scatter_dimension=1, tiled=True)
    gq, gwkv = attend_back(slots, queries, d_mixed, w_key, w_value, probs, mixing, db_count)
    high = db_count // low
    block = out_cols.shape[1] // high
    plane_wo = jnp.stack(
        [
            lax.dot_general(
                plane_mixed,
                out_cols[:, d * block:(d + 1) * block],
                (((0,), (0,)), ((), ())),
                preferred_element_type=F32,
            ).astype(BF16)
            for d in range(high)
        ]
    )
    grad_wv, grad_wk, grad_wo = reduce_scatter(gwkv, plane_wo)
    return (attended, gq, grad_wk, grad_wv, grad_wo)


def solution(mesh):
    placed = (
        P("db", "head"),
        P(None, "head"),
        P(None, "head"),
        P("head", None),
        P("db", "head", None),
        P("db", None),
        P("db", None),
        P("db"),
        P("db", "head"),
    )
    return jax.shard_map(
        shards,
        mesh=mesh,
        in_specs=placed,
        out_specs=(
            P("db", "head"),
            P("db", "head"),
            P("db", "head"),
            P("db", "head"),
            P("head", "db"),
        ),
        check_vma=False,
    )
```

```python
import functools
import itertools
import math

import jax
import jax.numpy as jnp
from jax import lax
from jax.experimental import pallas as pl
from jax.experimental.pallas import tpu as pltpu
from jax.sharding import PartitionSpec as P

HD = 128
F32 = jnp.float32
BF16 = jnp.bfloat16
VMEM_LIMIT = 56 * 1024 * 1024


def nt(a, b):
    return lax.dot_general(a, b, (((1,), (1,)), ((), ())), preferred_element_type=F32)


def nn(a, b):
    return jnp.dot(a, b, preferred_element_type=F32)


def tn(a, b):
    return lax.dot_general(a, b, (((0,), (0,)), ((), ())), preferred_element_type=F32)


def forward_kernel(groups, heads, count_ref, slots_ref, q_ref, wk_ref, wv_ref,
                   mixed_ref, probs_ref, pulled_ref):
    tokens = q_ref.shape[0] // groups
    key_len = slots_ref.shape[1]
    tokens_per_slot = key_len // 8
    factor = 1.0 / math.sqrt(HD)
    for c in range(groups):
        rows = slice(c * tokens, (c + 1) * tokens)
        slots = slots_ref[c]
        lifted = jnp.concatenate(
            [
                nt(q_ref[rows, h * HD:(h + 1) * HD], wk_ref[:, h * HD:(h + 1) * HD]).astype(BF16)
                for h in range(heads)
            ],
            axis=0,
        )
        scores = nt(lifted, slots) * factor
        position = lax.broadcasted_iota(jnp.int32, (1, key_len), 1)
        live = position < count_ref[c] * tokens_per_slot
        expo = jnp.where(live, jnp.exp(scores), 0.0)
        probs = (expo / jnp.sum(expo, axis=-1, keepdims=True)).astype(BF16)
        probs_ref[0, c] = probs
        pulled = nn(probs, slots).astype(BF16)
        for h in range(heads):
            part = pulled[h * tokens:(h + 1) * tokens]
            cols = slice(h * HD, (h + 1) * HD)
            mixed_ref[rows, cols] = nn(part, wv_ref[:, cols]).astype(BF16)
            pulled_ref[h, rows, :] = part


def backward_kernel(groups, heads, shares, slots_ref, q_ref, dm_ref, wk_ref, wv_ref, probs_ref,
                    mixing_ref, gq_ref, gwkv_ref, pulled_ref):
    tokens = q_ref.shape[0] // groups
    factor = 1.0 / math.sqrt(HD)
    for c in range(groups):
        rows = slice(c * tokens, (c + 1) * tokens)
        slots = slots_ref[c]
        lifted = jnp.concatenate(
            [
                nt(dm_ref[rows, h * HD:(h + 1) * HD], wv_ref[:, h * HD:(h + 1) * HD]).astype(BF16)
                for h in range(heads)
            ],
            axis=0,
        )
        d_probs = nt(lifted, slots)
        probs = probs_ref[0, c].astype(F32)
        weighted = probs * d_probs
        inner = jnp.sum(weighted, axis=-1, keepdims=True)
        d_scores = ((weighted - probs * inner) * factor).astype(BF16)
        pulled = nn(d_scores, slots).astype(BF16)
        for h in range(heads):
            part = pulled[h * tokens:(h + 1) * tokens]
            cols = slice(h * HD, (h + 1) * HD)
            gq_ref[rows, cols] = nn(part, wk_ref[:, cols]).astype(BF16)
            pulled_ref[h, rows, :] = part
    for h in range(heads):
        cols = slice(h * HD, (h + 1) * HD)
        of_value = tn(mixing_ref[h], dm_ref[:, cols])
        of_key = tn(pulled_ref[h], q_ref[:, cols])
        depth = of_key.shape[0] // shares
        for d in range(shares):
            part = slice(d * depth, (d + 1) * depth)
            both = jnp.concatenate([of_value[part], of_key[part]], axis=0)
            gwkv_ref[d, :, cols] = both.astype(BF16)


def attention_setup(slots, queries):
    groups, key_len, enc = slots.shape
    tok_rows, width = queries.shape
    heads = min(4, width // HD)
    steps = width // (heads * HD)
    part = heads * HD
    group_rows = heads * (tok_rows // groups)
    specs = dict(
        whole=pl.BlockSpec((groups, key_len, enc), lambda i: (0, 0, 0)),
        tok=pl.BlockSpec((tok_rows, part), lambda i: (0, i)),
        weight=pl.BlockSpec((enc, part), lambda i: (0, i)),
        prob=pl.BlockSpec((1, groups, group_rows, key_len), lambda i: (i, 0, 0, 0)),
        pull=pl.BlockSpec((heads, tok_rows, enc), lambda i: (i, 0, 0)),
    )
    shapes = dict(
        tok=jax.ShapeDtypeStruct((tok_rows, width), BF16),
        prob=jax.ShapeDtypeStruct((steps, groups, group_rows, key_len), BF16),
        pull=jax.ShapeDtypeStruct((width // HD, tok_rows, enc), BF16),
    )
    common = dict(
        grid=(steps,),
        compiler_params=pltpu.CompilerParams(vmem_limit_bytes=VMEM_LIMIT),
        cost_estimate=pl.CostEstimate(
            flops=int(4 * groups * group_rows * key_len * enc * steps * 1.2),
            bytes_accessed=20_000_000,
            transcendentals=groups * group_rows * steps * key_len,
        ),
    )
    return groups, heads, specs, shapes, common


def attend(slots, queries, w_key, w_value, nbr_count):
    groups, heads, specs, shapes, common = attention_setup(slots, queries)
    return pl.pallas_call(
        functools.partial(forward_kernel, groups, heads),
        in_specs=[pl.BlockSpec(memory_space=pltpu.SMEM)]
        + [specs[n] for n in ("whole", "tok", "weight", "weight")],
        out_specs=[specs[n] for n in ("tok", "prob", "pull")],
        out_shape=[shapes[n] for n in ("tok", "prob", "pull")],
        **common,
    )(nbr_count, slots, queries, w_key, w_value)


def attend_back(slots, queries, d_mixed, w_key, w_value, probs, mixing, shares):
    groups, heads, specs, shapes, common = attention_setup(slots, queries)
    tok_rows, width = queries.shape
    enc = slots.shape[2]
    rows = 2 * enc // shares
    return pl.pallas_call(
        functools.partial(backward_kernel, groups, heads, shares),
        in_specs=[specs[n] for n in ("whole", "tok", "tok", "weight", "weight", "prob", "pull")],
        out_specs=[
            specs["tok"],
            pl.BlockSpec((shares, rows, heads * HD), lambda i: (0, 0, i)),
        ],
        out_shape=[shapes["tok"], jax.ShapeDtypeStruct((shares, rows, width), BF16)],
        scratch_shapes=[pltpu.VMEM((heads, tok_rows, enc), BF16)],
        **common,
    )(slots, queries, d_mixed, w_key, w_value, probs, mixing)


class Track:
    def __init__(self, me, source, tail, order, buffers, buffer_tail, finish):
        self.me, self.cur, self.tail, self.order = me, source, tail, order
        self.bits = sorted(order, reverse=True)
        self.buffers, self.buffer_tail, self.finish = buffers, buffer_tail, finish
        self.stage = 0
        self.copy = None

    def start(self, send_sem, recv_sem):
        bit = self.order[self.stage]
        mine = lax.rem(self.me // (1 << bit), 2)
        lead = [slice(None)] * len(self.bits)
        lead[self.bits.index(bit)] = 1 - mine
        free = (slice(None),) * (len(self.bits) - 1)
        self.copy = pltpu.make_async_remote_copy(
            src_ref=self.cur.at[tuple(lead) + self.tail],
            dst_ref=self.buffers[self.stage].at[free + self.buffer_tail],
            send_sem=send_sem,
            recv_sem=recv_sem,
            device_id={"db": self.me + (1 - 2 * mine) * (1 << bit)},
            device_id_type=pl.DeviceIdType.MESH,
        )
        self.copy.start()
        return self.copy

    def add(self):
        self.copy.wait_recv()
        bit = self.order[self.stage]
        mine = lax.rem(self.me // (1 << bit), 2)
        place = self.bits.index(bit)
        buffer = self.buffers[self.stage]
        last = self.stage == len(self.order) - 1
        for rest in itertools.product(range(2), repeat=len(self.bits) - 1):
            keep = rest[:place] + (mine,) + rest[place:]
            total = self.cur[keep + self.tail].astype(F32) + buffer[
                rest + self.buffer_tail
            ].astype(F32)
            if last:
                self.finish(total)
            else:
                buffer[rest + self.buffer_tail] = total.astype(BF16)
        self.bits.remove(bit)
        self.cur, self.tail = buffer, self.buffer_tail
        self.stage += 1
        return last


def reduce_kernel(all_bits, wo_bits, kv_ref, wo_ref, gv_ref, gk_ref, gwo_ref, *scratch):
    me = lax.axis_index("db")
    kv_bufs = (scratch[0:all_bits], scratch[all_bits:2 * all_bits])
    at = 2 * all_bits
    wo_bufs = (scratch[at:at + wo_bits], scratch[at + wo_bits:at + 2 * wo_bits])
    send_sem, recv_sem = scratch[-2:]

    barrier = pltpu.get_barrier_semaphore()
    for bit in range(all_bits):
        mine = lax.rem(me // (1 << bit), 2)
        pl.semaphore_signal(
            barrier,
            inc=1,
            device_id={"db": me + (1 - 2 * mine) * (1 << bit)},
            device_id_type=pl.DeviceIdType.MESH,
        )
    pl.semaphore_wait(barrier, all_bits)

    depth = gv_ref.shape[0]
    half = kv_ref.shape[-1] // 2
    chunks = min(4, half // 128)
    size = half // chunks
    rows_half = wo_ref.shape[-2] // 2
    wo_size = rows_half // chunks
    rounds = []
    for c in range(chunks):
        pair = []
        rounds.append(pair)
        for t in range(2):
            order = list(range(all_bits))
            if t == 1:
                order[0], order[1] = order[1], order[0]
            cols = slice(t * half + c * size, t * half + (c + 1) * size)

            def finish(total, cols=cols):
                gv_ref[:, cols] = total[:depth]
                gk_ref[:, cols] = total[depth:]

            pair.append(
                Track(me, kv_ref, (slice(None), cols), order, kv_bufs[t],
                      (slice(None), slice(c * size, (c + 1) * size)), finish)
            )
        pair = []
        rounds.append(pair)
        for t in range(2):
            order = list(range(all_bits - wo_bits, all_bits))
            rows = slice(t * rows_half + c * wo_size, t * rows_half + (c + 1) * wo_size)

            def finish(total, rows=rows):
                gwo_ref[rows, :] = total

            pair.append(
                Track(me, wo_ref, (rows, slice(None)), order, wo_bufs[t],
                      (slice(c * wo_size, (c + 1) * wo_size), slice(None)), finish)
            )

    copies = []

    def start(track):
        k = len(copies)
        copies.append(track.start(send_sem.at[k], recv_sem.at[k]))

    for track in rounds[0]:
        start(track)
    active = []
    for t in range(len(rounds) + all_bits):
        active += rounds[t:t + 1]
        for pair in rounds[t + 1:t + 2]:
            for track in pair:
                start(track)
        for pair in list(active):
            for track in pair:
                if not track.add():
                    start(track)
                elif pair in active:
                    active.remove(pair)
    for copy in copies:
        copy.wait_send()


def reduce_scatter(gwkv, gwo):
    shares, rows, width = gwkv.shape
    low, out_rows, out_cols = gwo.shape
    all_bits, wo_bits = shares.bit_length() - 1, low.bit_length() - 1
    kv_half, wo_half = width // 2, out_rows // 2
    chunks = min(4, kv_half // 128)
    kv_bufs = [
        pltpu.VMEM((2,) * (all_bits - s - 1) + (rows, kv_half), BF16) for s in range(all_bits)
    ]
    wo_bufs = [
        pltpu.VMEM((2,) * (wo_bits - s - 1) + (wo_half, out_cols), BF16) for s in range(wo_bits)
    ]
    n_copies = 2 * chunks * (all_bits + wo_bits)
    in_vmem = pl.BlockSpec(memory_space=pltpu.VMEM)
    return pl.pallas_call(
        functools.partial(reduce_kernel, all_bits, wo_bits),
        in_specs=[in_vmem, in_vmem],
        out_specs=[in_vmem] * 3,
        out_shape=[
            jax.ShapeDtypeStruct((rows // 2, width), F32),
            jax.ShapeDtypeStruct((rows // 2, width), F32),
            jax.ShapeDtypeStruct((out_rows, out_cols), F32),
        ],
        scratch_shapes=kv_bufs + kv_bufs + wo_bufs + wo_bufs
        + [pltpu.SemaphoreType.DMA((n_copies,)), pltpu.SemaphoreType.DMA((n_copies,))],
        compiler_params=pltpu.CompilerParams(
            collective_id=0, has_side_effects=True, vmem_limit_bytes=VMEM_LIMIT
        ),
        cost_estimate=pl.CostEstimate(
            flops=gwkv.size, bytes_accessed=300_000_000, transcendentals=0
        ),
    )(
        gwkv.reshape((2,) * all_bits + (rows, width)),
        gwo.reshape((2,) * wo_bits + (out_rows, out_cols)),
    )


def remote(source, target, send_sem, recv_sem, device):
    copy = pltpu.make_async_remote_copy(
        src_ref=source,
        dst_ref=target,
        send_sem=send_sem,
        recv_sem=recv_sem,
        device_id=device,
        device_id_type=pl.DeviceIdType.MESH,
    )
    copy.start()
    return copy


def greet(db_peers, head_peers):
    barrier = pltpu.get_barrier_semaphore()
    for device in [{"db": d} for d in db_peers] + [{"head": h} for h in head_peers]:
        pl.semaphore_signal(barrier, inc=1, device_id=device,
                            device_id_type=pl.DeviceIdType.MESH)
    pl.semaphore_wait(barrier, len(db_peers) + len(head_peers))


def request_kernel(wanted_ref, incoming_ref, send_sem, recv_sem):
    db_count, me = lax.axis_size("db"), lax.axis_index("db")
    peers = [lax.rem(me + k, db_count) for k in range(1, db_count)]
    greet(peers, [])
    copies = [
        remote(wanted_ref.at[to], incoming_ref.at[me], send_sem.at[n], recv_sem.at[n], {"db": to})
        for n, to in enumerate(peers)
    ]
    incoming_ref[me] = wanted_ref[me]
    for copy in copies:
        copy.wait()


def exchange_kernel(low, grad_ref, piece_ref, cols_ref, send_sem, recv_sem):
    db_count, head_count = lax.axis_size("db"), lax.axis_size("head")
    me, head = lax.axis_index("db"), lax.axis_index("head")
    tokens, width = grad_ref.shape
    high = db_count // low
    block = width * head_count // db_count
    lower, upper = lax.rem(me, low), me // low
    near = [lax.rem(lower + k, low) for k in range(1, low)]
    heads = [lax.rem(head + k, head_count) for k in range(1, head_count)]
    greet([upper * low + to for to in near], heads)
    copies = []
    own = pl.ds(pl.multiple_of(head * width, width), width)
    for to in heads:
        n = len(copies)
        copies.append(remote(grad_ref, piece_ref.at[:, own], send_sem.at[n], recv_sem.at[n],
                             {"head": to}))
    piece_ref[:, own] = grad_ref[...]
    for copy in copies:
        copy.wait_recv()
    rows = pl.ds(pl.multiple_of(lower * tokens, tokens), tokens)
    for to in near:
        for u in range(high):
            n = len(copies)
            cols = pl.ds(pl.multiple_of((u * low + to) * block, block), block)
            copies.append(remote(piece_ref.at[:, cols],
                                 cols_ref.at[rows, u * block:(u + 1) * block],
                                 send_sem.at[n], recv_sem.at[n], {"db": upper * low + to}))
    for u in range(high):
        cols = pl.ds(pl.multiple_of((u * low + lower) * block, block), block)
        cols_ref[rows, u * block:(u + 1) * block] = piece_ref[:, cols]
    for copy in copies[head_count - 1:]:
        copy.wait_recv()
    for copy in copies:
        copy.wait_send()


def request(wanted):
    n = lax.axis_size("db") - 1
    in_vmem = pl.BlockSpec(memory_space=pltpu.VMEM)
    return pl.pallas_call(
        request_kernel,
        in_specs=[in_vmem],
        out_specs=in_vmem,
        out_shape=jax.ShapeDtypeStruct(wanted.shape, jnp.int32),
        scratch_shapes=[pltpu.SemaphoreType.DMA((n,)), pltpu.SemaphoreType.DMA((n,))],
        compiler_params=pltpu.CompilerParams(collective_id=3, has_side_effects=True),
    )(wanted)


def exchange(grad_out, low):
    db_count, head_count = lax.axis_size("db"), lax.axis_size("head")
    tokens, width = grad_out.shape
    full = width * head_count
    n = head_count - 1 + (low - 1) * (db_count // low)
    in_vmem = pl.BlockSpec(memory_space=pltpu.VMEM)
    return pl.pallas_call(
        functools.partial(exchange_kernel, low),
        in_specs=[in_vmem],
        out_specs=[in_vmem] * 2,
        out_shape=[
            jax.ShapeDtypeStruct((tokens, full), BF16),
            jax.ShapeDtypeStruct((low * tokens, full // low), BF16),
        ],
        scratch_shapes=[pltpu.SemaphoreType.DMA((n,)), pltpu.SemaphoreType.DMA((n,))],
        compiler_params=pltpu.CompilerParams(
            collective_id=1, has_side_effects=True, vmem_limit_bytes=VMEM_LIMIT
        ),
        cost_estimate=pl.CostEstimate(flops=0, bytes_accessed=40_000_000, transcendentals=0),
    )(grad_out)


def share_kernel(mine_ref, whole_ref, send_sem, recv_sem, local_sem):
    head_count, head = lax.axis_size("head"), lax.axis_index("head")
    depth = mine_ref.shape[1]
    barrier = pltpu.get_barrier_semaphore()
    for k in range(1, head_count):
        pl.semaphore_signal(barrier, inc=1, device_id={"head": lax.rem(head + k, head_count)},
                            device_id_type=pl.DeviceIdType.MESH)
    pl.semaphore_wait(barrier, head_count - 1)
    place = whole_ref.at[:, pl.ds(pl.multiple_of(head * depth, depth), depth), :]
    copies = [
        remote(mine_ref, place, send_sem.at[k - 1], recv_sem.at[k - 1],
               {"head": lax.rem(head + k, head_count)})
        for k in range(1, head_count)
    ]
    local = pltpu.make_async_copy(mine_ref, place, local_sem)
    local.start()
    for copy in copies:
        copy.wait()
    local.wait()


def share(mine):
    head_count = lax.axis_size("head")
    rows, depth, enc = mine.shape
    in_vmem = pl.BlockSpec(memory_space=pltpu.VMEM)
    return pl.pallas_call(
        share_kernel,
        in_specs=[in_vmem],
        out_specs=in_vmem,
        out_shape=jax.ShapeDtypeStruct((rows, depth * head_count, enc), BF16),
        scratch_shapes=[
            pltpu.SemaphoreType.DMA((head_count - 1,)),
            pltpu.SemaphoreType.DMA((head_count - 1,)),
            pltpu.SemaphoreType.DMA,
        ],
        compiler_params=pltpu.CompilerParams(
            collective_id=2, has_side_effects=True, vmem_limit_bytes=VMEM_LIMIT
        ),
    )(mine)


def shards(queries, w_key, w_value, w_out, encodings, nbr_row, nbr_owner, nbr_count, grad_out):
    db_count = lax.axis_size("db")
    head_count = lax.axis_size("head")
    groups, slot_count = nbr_row.shape
    tok_rows, local_width = queries.shape
    enc_width = encodings.shape[2]
    slice_len = encodings.shape[1]
    owner_ids = lax.broadcasted_iota(jnp.int32, (1, 1, db_count), 2)
    chosen = nbr_owner[:, :, None] == owner_ids
    wanted = jnp.sum(jnp.where(chosen, nbr_row[:, :, None], 0), axis=1)
    low = 1 << ((db_count.bit_length() - 1) // 2)
    planes = [list(range(first, first + low)) for first in range(0, db_count, low)]
    padded = jnp.broadcast_to(
        jnp.pad(wanted.T, ((0, 0), (0, 128 - groups)))[:, None, :], (db_count, 8, 128)
    )
    incoming = request(padded)
    table = jnp.take(encodings, incoming[:, 0, :groups].reshape(-1), axis=0, mode="clip")
    table = table.reshape(db_count, groups * slice_len, enc_width)
    received = lax.all_to_all(table, "db", split_axis=0, concat_axis=0, tiled=True)
    piece, out_cols = exchange(lax.optimization_barrier((grad_out, table))[0], low)
    d_mixed = lax.dot_general(
        piece, w_out, (((1,), (1,)), ((), ())), preferred_element_type=F32
    ).astype(BF16)
    received, d_mixed, out_cols = lax.optimization_barrier((received, d_mixed, out_cols))
    received = received.reshape(db_count * groups, slice_len, enc_width)
    picks = nbr_owner * groups + lax.broadcasted_iota(jnp.int32, nbr_owner.shape, 0)
    mine = jnp.take(received, picks.reshape(-1), axis=0, mode="clip")
    slots = share(mine).reshape(groups, slot_count * slice_len * head_count, enc_width)
    mixed, probs, mixing = attend(slots, queries, w_key, w_value, nbr_count)
    plane_mixed = lax.all_gather(mixed, "db", axis=0, axis_index_groups=planes, tiled=True)
    out_term = jnp.dot(mixed, w_out, preferred_element_type=F32)
    attended = lax.psum_scatter(out_term.astype(BF16), "head", scatter_dimension=1, tiled=True)
    gq, gwkv = attend_back(slots, queries, d_mixed, w_key, w_value, probs, mixing, db_count)
    high = db_count // low
    block = out_cols.shape[1] // high
    plane_wo = jnp.stack(
        [
            lax.dot_general(
                plane_mixed,
                out_cols[:, d * block:(d + 1) * block],
                (((0,), (0,)), ((), ())),
                preferred_element_type=F32,
            ).astype(BF16)
            for d in range(high)
        ]
    )
    grad_wv, grad_wk, grad_wo = reduce_scatter(gwkv, plane_wo)
    return (attended, gq, grad_wk, grad_wv, grad_wo)


def solution(mesh):
    placed = (
        P("db", "head"),
        P(None, "head"),
        P(None, "head"),
        P("head", None),
        P("db", "head", None),
        P("db", None),
        P("db", None),
        P("db"),
        P("db", "head"),
    )
    return jax.shard_map(
        shards,
        mesh=mesh,
        in_specs=placed,
        out_specs=(
            P("db", "head"),
            P("db", "head"),
            P("db", "head"),
            P("db", "head"),
            P("head", "db"),
        ),
        check_vma=False,
    )
```
